256 devices in a mesh: stream: 16 (over y_hi, x, core), span: 16 (over y_lo, z).
Axes of the slice: x: 4, y: 4 (y_hi: 2, y_lo: 2; y = y_hi * 2 + y_lo), z: 8, core: 2. Of those that a mesh axis runs over, the one named last changes fastest.
Arguments:
- rhs: float32 [16, 160, 64, 320], P('stream', 'span'), may hold values from -6 to 6
- dinv: bfloat16 [16, 160, 320, 320], P('stream', 'span'), may hold values from -0.04528038 to 1.1552804
- lower_up: bfloat16 [16, 160, 320, 320], P('stream', 'span'), may hold values from -0.29492188 to 0.29492188
- lower_span: bfloat16 [16, 80, 2, 320, 320], P('stream', 'span'), may hold values from -0.083496094 to 0.083496094
- upper_down: bfloat16 [16, 160, 320, 320], P('stream', 'span'), may hold values from -0.29492188 to 0.29492188
- upper_span: bfloat16 [16, 80, 2, 320, 320], P('stream', 'span'), may hold values from -0.083496094 to 0.083496094
- span_link: int32 [16, 160], P('stream', 'span'), may hold values 0 or 1
Outputs:
- preconditioned: float32 [16, 160, 64, 320], P('stream', 'span')
The draws below stay inside these ranges and needn't reach their ends.
All inputs are finite; a program needn't handle non-finite values. No bound on the sum of `span_link` on one device may be relied on, other than what follows from the above.
Results may differ from the reference program's by a relative error of at most 0.035.
Values may be sent and summed in bfloat16 or wider, within the bound.
No kernel may reach another device: no remote copies, remote signals or barrier semaphores. Data moves between devices by JAX's collectives and lax.ppermute only.
A program may use at most 64 MiB of HBM per device.

```python
import math
import jax
import jax.numpy as jnp
from jax import lax

BLOCK = 320
VECS = 64
LAYERS = 16
SPAN_CELLS = 160


def draw_dinv(key, part):
    scale_key, noise_key = jax.random.split(jax.random.fold_in(key, 7))
    shape = (LAYERS, SPAN_CELLS, BLOCK, BLOCK)
    diagonal_scale = 0.7 + 0.4 * jax.random.uniform(scale_key, (LAYERS, SPAN_CELLS, BLOCK, 1), jnp.float32)
    noise = jnp.clip(jax.random.normal(noise_key, shape, jnp.float32), -4.0, 4.0)
    identity = jnp.eye(BLOCK, dtype=jnp.float32)
    return (identity * diagonal_scale + noise * (0.2 / math.sqrt(BLOCK))).astype(jnp.bfloat16)


def touch_ends(array, rng, smallest, largest):
    place = [jax.random.randint(jax.random.fold_in(rng, axis), (), 0, length) for axis, length in enumerate(array.shape)]
    longest = array.shape.index(max(array.shape))
    next_to = place[:longest] + [(place[longest] + 1) % array.shape[longest]] + place[longest + 1:]
    return array.at[tuple(place)].set(smallest).at[tuple(next_to)].set(largest)


def block_levels(key, extent, pieces, smallest, largest):
    level = 1.0
    for position, shards_of in pieces:
        draws = jax.random.uniform(jax.random.fold_in(jax.random.fold_in(key, 6), position), (shards_of,), jnp.float32, smallest / len(pieces), largest / len(pieces))
        level = level * jnp.repeat(jnp.exp(draws), extent[position] // shards_of).reshape((-1,) + (1,) * (len(extent) - 1 - position))
    return level


def scatter_about(rng, dims, scale, reach, pieces=(), kind=jnp.bfloat16):
    array = jax.random.normal(rng, dims, jnp.float32) * scale
    if len(pieces) > 0:
        array = block_levels(rng, dims, pieces, -0.22, 0.18) * array
    return jnp.clip(array, min=-reach, max=reach).astype(kind)


def setup_inputs(seed: int = 0) -> dict:
    streams_of = jax.random.split(jax.random.key(seed), 8)
    rhs = scatter_about(streams_of[0], (LAYERS, SPAN_CELLS, VECS, BLOCK), 1.0, 6.0, ((0, 16), (1, 16)), jnp.float32)
    dinv = draw_dinv(jax.random.fold_in(streams_of[7], 71), 0)
    lower_up = scatter_about(streams_of[2], (LAYERS, SPAN_CELLS, BLOCK, BLOCK), (0.88 / BLOCK ** 0.5), 0.29492188, ((0, 16), (1, 16)))
    lower_span = scatter_about(streams_of[3], (LAYERS, SPAN_CELLS // 2, 2, BLOCK, BLOCK), (0.25 / BLOCK ** 0.5), 0.083496094, ((0, 16), (1, 16)))
    upper_down = scatter_about(streams_of[4], (LAYERS, SPAN_CELLS, BLOCK, BLOCK), (0.88 / BLOCK ** 0.5), 0.29492188, ((0, 16), (1, 16)))
    upper_span = scatter_about(streams_of[5], (LAYERS, SPAN_CELLS // 2, 2, BLOCK, BLOCK), (0.25 / BLOCK ** 0.5), 0.083496094, ((0, 16), (1, 16)))
    span_link = touch_ends((jax.random.randint(streams_of[6], (LAYERS, SPAN_CELLS), 0, 4) < 3).astype(jnp.int32), jax.random.fold_in(streams_of[6], 1), 0, 1)
    return {"rhs": rhs, "dinv": dinv, "lower_up": lower_up, "lower_span": lower_span, "upper_down": upper_down, "upper_span": upper_span, "span_link": span_link}


def apply_blocks(blocks, vectors):
    rounded = lax.optimization_barrier(vectors.astype(jnp.bfloat16))
    return jnp.einsum("cij,cvj->cvi", blocks.astype(jnp.float32), rounded.astype(jnp.float32), precision=lax.Precision.HIGHEST)


def reference(rhs, dinv, lower_up, lower_span, upper_down, upper_span, span_link):
    pair_count = SPAN_CELLS // 2
    links = span_link.astype(jnp.float32).reshape(LAYERS, pair_count, 2)
    empty_cell = jnp.zeros((1, VECS, BLOCK), jnp.float32)
    upstream = jnp.zeros((pair_count, 2, VECS, BLOCK), jnp.float32)
    forward_rows = []
    for layer in range(LAYERS):
        source = rhs[layer].reshape(pair_count, 2, VECS, BLOCK)
        coupling = lower_up[layer].reshape(pair_count, 2, BLOCK, BLOCK)
        even_part = source[:, 0] - apply_blocks(coupling[:, 0], upstream[:, 0])
        beyond = jnp.concatenate([even_part[1:], empty_cell], axis=0)
        odd_part = source[:, 1] - apply_blocks(coupling[:, 1], upstream[:, 1])
        odd_part = odd_part - links[layer, :, 0][:, None, None] * apply_blocks(lower_span[layer, :, 0], even_part)
        odd_part = odd_part - links[layer, :, 1][:, None, None] * apply_blocks(lower_span[layer, :, 1], beyond)
        upstream = jnp.stack([even_part, odd_part], axis=1)
        forward_rows.append(upstream)
    downstream = jnp.zeros((pair_count, 2, VECS, BLOCK), jnp.float32)
    results = [None] * LAYERS
    for layer in reversed(range(LAYERS)):
        current = forward_rows[layer]
        coupling = upper_down[layer].reshape(pair_count, 2, BLOCK, BLOCK)
        inverse = dinv[layer].reshape(pair_count, 2, BLOCK, BLOCK)
        odd_part = apply_blocks(inverse[:, 1], current[:, 1] - apply_blocks(coupling[:, 1], downstream[:, 1]))
        left_link = jnp.concatenate([jnp.zeros((1,), jnp.float32), links[layer, :-1, 1]])
        before = jnp.concatenate([empty_cell, odd_part[:-1]], axis=0)
        reduced = current[:, 0] - apply_blocks(coupling[:, 0], downstream[:, 0])
        reduced = reduced - left_link[:, None, None] * apply_blocks(upper_span[layer, :, 0], before)
        reduced = reduced - links[layer, :, 0][:, None, None] * apply_blocks(upper_span[layer, :, 1], odd_part)
        even_part = apply_blocks(inverse[:, 0], reduced)
        downstream = jnp.stack([even_part, odd_part], axis=1)
        results[layer] = downstream.reshape(SPAN_CELLS, VECS, BLOCK)
    return jnp.stack(results, axis=0)
```

```python
import functools
import jax
import jax.numpy as jnp
from jax import lax
from jax.experimental import pallas as pl
from jax.experimental.pallas import tpu as pltpu
from jax.sharding import PartitionSpec as P

F32 = jnp.float32
BF16 = jnp.bfloat16
LIMIT = 24 * 1024 * 1024

EVEN_LOW, EVEN_HIGH, ODD_LOW, ODD_HIGH, ODD_PART, ODD_INFLOW = range(6)
REST_LOW, REST_HIGH, OUT_ODD_LOW, OUT_ODD_HIGH, GAIN_LOW, GAIN_HIGH, OUT_EVEN_LOW, EVEN_INFLOW = range(8)


def times(vectors, block):
    return lax.dot_general(
        vectors.astype(BF16), block, (((1,), (1,)), ((), ())), preferred_element_type=F32
    )


def product(left, right):
    return lax.dot_general(left, right, (((1,), (0,)), ((), ())), preferred_element_type=F32)


def run(body, outs, *operands, alias=None, hbm=(), scratch=()):
    in_vmem = pl.BlockSpec(memory_space=pltpu.VMEM)
    in_hbm = pl.BlockSpec(memory_space=pltpu.HBM)
    return pl.pallas_call(
        body,
        out_shape=[pltpu.VMEM(shape, dtype) for shape, dtype in outs],
        in_specs=[in_hbm if index in hbm else in_vmem for index in range(len(operands))],
        out_specs=[in_vmem] * len(outs),
        input_output_aliases=alias or {},
        scratch_shapes=list(scratch),
        compiler_params=pltpu.CompilerParams(vmem_limit_bytes=LIMIT),
    )(*operands)


def place():
    stream = lax.axis_index("stream")
    return stream // 2, stream % 2


def ordered(active, core, own, other, work):
    @pl.when(active & (core == 0))
    def _():
        work(own, other)

    @pl.when(active & (core == 1))
    def _():
        work(other, own)


def half_rows(core, half):
    return pl.ds(pl.multiple_of(core * half, half), half)


def pack_kernel(rhs, link, own, sent, whole_link, own_sem, sent_sem, link_sem):
    _, core = place()
    cells, half, width = own.shape[0] - 1, own.shape[1], own.shape[2]
    copies = [
        pltpu.make_async_copy(
            rhs.at[:, half_rows(1 - core, half), :], sent.at[pl.ds(0, cells)], sent_sem
        ),
        pltpu.make_async_copy(link, whole_link, link_sem),
        pltpu.make_async_copy(
            rhs.at[:, half_rows(core, half), :], own.at[pl.ds(0, cells)], own_sem
        ),
    ]
    for copy in copies:
        copy.start()
    for copy in copies:
        copy.wait()
    for packed in (own, sent):
        packed[cells] = jnp.zeros((half, width), F32)
        packed[cells, 0:1, 0:cells] = whole_link[...].astype(F32)


def first_kernel(source, source_x, lower, lower_x, state, out):
    _, core = place()
    pairs = out.shape[0]

    def work(low, high):
        for pair in range(pairs):
            fresh = high[0][2 * pair] - times(low[0][2 * pair], high[1][2 * pair])
            out[pair] = fresh.astype(BF16)
            state[EVEN_HIGH, pair] = fresh
        for pair in range(pairs):
            state[EVEN_LOW, pair] = low[0][2 * pair]

    ordered(True, core, (source, lower), (source_x, lower_x), work)


def ahead_kernel(lower, lower_x, inverse, upper, both, chain):
    stage, core = place()

    def work(low, high):
        for cell in range(lower.shape[0]):
            both[cell] = product(high[cell], low[cell]).astype(BF16)

    ordered(stage > 0, core, lower, lower_x, work)

    @pl.when(stage > 0)
    def _():
        for cell in range(inverse.shape[0]):
            chain[cell] = product(inverse[cell], upper[cell]).astype(BF16)


def chain_kernel(inverse, upper, state_in, chain_in, chain):
    stage, _ = place()

    @pl.when(stage == 0)
    def _():
        for cell in range(inverse.shape[0]):
            chain[cell] = product(inverse[cell], upper[cell]).astype(BF16)


def back_product_kernel(last, chain, chain_x, both):
    stage, core = place()

    def work(low, high):
        for cell in range(chain.shape[0]):
            both[cell] = product(low[cell], high[cell]).astype(BF16)

    ordered(stage < last, core, chain, chain_x, work)


def even_kernel(turn, recv, both, state_in, state, out):
    stage, _ = place()

    @pl.when(stage == turn)
    def _():
        for pair in range(out.shape[0]):
            fresh = state[EVEN_HIGH, pair] + times(recv[pair], both[2 * pair])
            out[pair] = fresh.astype(BF16)
            state[EVEN_HIGH, pair] = fresh


def heads_kernel(turn, recv, lower, lower_x, state_in, state, heads):
    stage, core = place()

    def work(low, high):
        state[EVEN_LOW, 0] = state[EVEN_LOW, 0] - times(recv[0], low[0])
        heads[0] = state[EVEN_LOW, 0].astype(BF16)
        heads[1] = state[EVEN_HIGH, 0].astype(BF16)

    ordered(stage == turn, core, lower, lower_x, work)


def first_heads_kernel(state_in, state, heads):
    heads[0] = state[EVEN_LOW, 0].astype(BF16)
    heads[1] = state[EVEN_HIGH, 0].astype(BF16)


def link_of(source, cell):
    cells = source.shape[0] - 1
    return source[cells, 0:1, cell : cell + 1]


def odd_source_kernel(
    turn, recv, source, source_x, lower, lower_x, side, side_x, state_in, state
):
    stage, core = place()
    pairs = side.shape[0]

    def work(low, high):
        if turn > 0:
            for pair in range(1, pairs):
                state[EVEN_LOW, pair] = state[EVEN_LOW, pair] - times(
                    recv[pair], low[1][2 * pair]
                )
        for layer, (values, _, sides) in enumerate((low, high)):
            even, odd = ((EVEN_LOW, ODD_LOW), (EVEN_HIGH, ODD_PART))[layer]
            for pair in range(pairs):
                fresh = values[2 * pair + 1]
                fresh = fresh - link_of(values, 2 * pair) * times(
                    state[even, pair], sides[pair, 0]
                )
                if pair + 1 < pairs:
                    fresh = fresh - link_of(values, 2 * pair + 1) * times(
                        state[even, pair + 1], sides[pair, 1]
                    )
                state[odd, pair] = fresh
        for pair in range(pairs - 1):
            state[ODD_PART, pair] = state[ODD_PART, pair] - times(
                state[ODD_LOW, pair], high[1][2 * pair + 1]
            )

    ordered(stage == turn, core, (source, lower, side), (source_x, lower_x, side_x), work)


def odd_last_kernel(
    turn, heads, source, source_x, lower, lower_x, side, side_x, state_in, state
):
    stage, core = place()
    pair = side.shape[0] - 1

    def work(low, high):
        for layer, (values, _, sides) in enumerate((low, high)):
            odd = (ODD_LOW, ODD_PART)[layer]
            state[odd, pair] = state[odd, pair] - link_of(values, 2 * pair + 1) * times(
                heads[layer], sides[pair, 1]
            )
        state[ODD_PART, pair] = state[ODD_PART, pair] - times(
            state[ODD_LOW, pair], high[1][2 * pair + 1]
        )

    ordered(stage == turn, core, (source, lower, side), (source_x, lower_x, side_x), work)


def odd_kernel(turn, recv, both, state_in, state, out):
    stage, _ = place()

    @pl.when(stage == turn)
    def _():
        for pair in range(out.shape[0]):
            fresh = state[ODD_PART, pair] + times(recv[pair], both[2 * pair + 1])
            out[pair] = fresh.astype(BF16)
            state[ODD_HIGH, pair] = fresh
            state[ODD_INFLOW, pair] = recv[pair].astype(F32)


def first_odd_kernel(state_in, state, out):
    for pair in range(out.shape[0]):
        fresh = state[ODD_PART, pair]
        out[pair] = fresh.astype(BF16)
        state[ODD_HIGH, pair] = fresh
        state[ODD_INFLOW, pair] = jnp.zeros(fresh.shape, F32)


def turn_back_kernel(forward, lower, lower_x, inverse, inverse_x, chain, chain_x, state, out):
    _, core = place()
    pairs = out.shape[0]

    def work(low, high):
        for pair in range(pairs):
            cell = 2 * pair + 1
            high_rest = times(forward[ODD_HIGH, pair], high[1][cell])
            low_value = forward[ODD_LOW, pair] - times(forward[ODD_INFLOW, pair], low[0][cell])
            low_rest = times(low_value, low[1][cell]) - times(high_rest, low[2][cell])
            state[REST_HIGH, pair] = high_rest
            state[OUT_ODD_HIGH, pair] = high_rest
            state[REST_LOW, pair] = low_rest
            state[OUT_ODD_LOW, pair] = low_rest
            out[pair] = low_rest.astype(BF16)

    ordered(True, core, (lower, inverse, chain), (lower_x, inverse_x, chain_x), work)


def odd_low_kernel(stage_of_turn, recv, both, state_in, state, out):
    stage, _ = place()

    @pl.when(stage == stage_of_turn)
    def _():
        for pair in range(out.shape[0]):
            fresh = state[REST_LOW, pair] + times(recv[pair], both[2 * pair + 1])
            out[pair] = fresh.astype(BF16)
            state[OUT_ODD_LOW, pair] = fresh


def even_out_kernel(stage_of_turn, recv, both, state_in, state, out):
    stage, _ = place()

    @pl.when(stage == stage_of_turn)
    def _():
        for pair in range(out.shape[0]):
            fresh = state[GAIN_LOW, pair] + times(recv[pair], both[2 * pair])
            out[pair] = fresh.astype(BF16)
            state[OUT_EVEN_LOW, pair] = fresh
            state[EVEN_INFLOW, pair] = recv[pair].astype(F32)


def first_even_out_kernel(state_in, state, out):
    for pair in range(out.shape[0]):
        fresh = state[GAIN_LOW, pair]
        out[pair] = fresh.astype(BF16)
        state[OUT_EVEN_LOW, pair] = fresh
        state[EVEN_INFLOW, pair] = jnp.zeros(fresh.shape, F32)


def tails_of(low, high, state, tails):
    pairs = state.shape[1]
    for layer, (values, row) in enumerate(((low, OUT_ODD_LOW), (high, OUT_ODD_HIGH))):
        tails[layer] = (state[row, pairs - 1] * link_of(values, 2 * pairs - 1)).astype(BF16)


def tails_kernel(
    stage_of_turn, recv, source, source_x, chain, chain_x, state_in, state, tails
):
    stage, core = place()
    pair = recv.shape[0] - 1

    def work(low, high):
        state[OUT_ODD_HIGH, pair] = state[REST_HIGH, pair] - times(
            recv[pair], high[1][2 * pair + 1]
        )
        tails_of(low[0], high[0], state, tails)

    ordered(stage == stage_of_turn, core, (source, chain), (source_x, chain_x), work)


def first_tails_kernel(source, source_x, state_in, state, tails):
    _, core = place()
    ordered(
        True, core, source, source_x, lambda low, high: tails_of(low, high, state, tails)
    )


def settle_gain(state, low, high, pair):
    high_gain = times(state[GAIN_HIGH, pair], high[1][2 * pair])
    low_gain = times(state[GAIN_LOW, pair], low[1][2 * pair])
    state[GAIN_HIGH, pair] = high_gain
    state[GAIN_LOW, pair] = low_gain - times(high_gain, low[2][2 * pair])


def even_gain_kernel(
    stage_of_turn, first, recv, source, source_x, forward, side, side_x, inverse, inverse_x,
    chain, chain_x, state_in, state
):
    stage, core = place()
    pairs = side.shape[0]

    def work(low, high):
        if not first:
            for pair in range(pairs - 1):
                state[OUT_ODD_HIGH, pair] = state[REST_HIGH, pair] - times(
                    recv[pair], high[2][2 * pair + 1]
                )
        for layer, (sides, _, _, values) in enumerate((low, high)):
            even, odd, gain = (
                (EVEN_LOW, OUT_ODD_LOW, GAIN_LOW),
                (EVEN_HIGH, OUT_ODD_HIGH, GAIN_HIGH),
            )[layer]
            for pair in range(pairs):
                fresh = forward[even, pair]
                if pair > 0:
                    fresh = fresh - link_of(values, 2 * pair - 1) * times(
                        state[odd, pair - 1], sides[pair, 0]
                    )
                fresh = fresh - link_of(values, 2 * pair) * times(
                    state[odd, pair], sides[pair, 1]
                )
                state[gain, pair] = fresh
        for pair in range(1, pairs):
            settle_gain(state, low, high, pair)

    ordered(
        stage == stage_of_turn, core,
        (side, inverse, chain, source), (side_x, inverse_x, chain_x, source_x), work,
    )


def even_first_kernel(
    stage_of_turn, tails, side, side_x, inverse, inverse_x, chain, chain_x, state_in, state
):
    stage, core = place()

    def work(low, high):
        for layer, (sides, _, _) in enumerate((low, high)):
            gain = (GAIN_LOW, GAIN_HIGH)[layer]
            state[gain, 0] = state[gain, 0] - times(tails[layer], sides[0, 0])
        settle_gain(state, low, high, 0)

    ordered(
        stage == stage_of_turn, core,
        (side, inverse, chain), (side_x, inverse_x, chain_x), work,
    )


def split_kernel(state, chain, chain_x, kept, sent):
    _, core = place()
    pairs = state.shape[1]

    def work(low, high):
        for pair in range(pairs):
            even_high = state[GAIN_HIGH, pair] - times(
                state[EVEN_INFLOW, pair], high[2 * pair]
            )
            if low is chain:
                kept[2 * pair] = state[OUT_EVEN_LOW, pair]
                kept[2 * pair + 1] = state[OUT_ODD_LOW, pair]
                sent[2 * pair] = even_high.astype(BF16)
                sent[2 * pair + 1] = state[OUT_ODD_HIGH, pair].astype(BF16)
            else:
                sent[2 * pair] = state[OUT_EVEN_LOW, pair].astype(BF16)
                sent[2 * pair + 1] = state[OUT_ODD_LOW, pair].astype(BF16)
                kept[2 * pair] = even_high
                kept[2 * pair + 1] = state[OUT_ODD_HIGH, pair]

    ordered(True, core, chain, chain_x, work)


def join_kernel(kept, arrived, result):
    _, core = place()
    cells, half = kept.shape[0], kept.shape[1]
    for cell in range(cells):
        result[cell, half_rows(core, half), :] = kept[cell]
        result[cell, half_rows(1 - core, half), :] = arrived[cell].astype(F32)


def shards(rhs, dinv, lower_up, lower_span, upper_down, upper_span, span_link):
    rhs, dinv, lower_up = rhs[0], dinv[0], lower_up[0]
    lower_span, upper_down, upper_span = lower_span[0], upper_down[0], upper_span[0]
    cells, vecs, width = rhs.shape
    pairs, half = cells // 2, vecs // 2
    streams, spans = lax.axis_size("stream"), lax.axis_size("span")
    last = streams // 2 - 1

    def swapped(value):
        return lax.ppermute(value, "stream", [(index, index ^ 1) for index in range(streams)])

    def hop(value, start, end):
        return lax.ppermute(
            value, "stream", [(2 * start + core, 2 * end + core) for core in (0, 1)]
        )

    def beside(value, stage, step):
        links = []
        for core in (0, 1):
            for span in range(spans):
                if 0 <= span + step < spans:
                    base = (2 * stage + core) * spans + span
                    links.append((base, base + step))
        return lax.ppermute(value, ("stream", "span"), links)

    def after(value, *others):
        return lax.optimization_barrier((value,) + others)[0]

    part = functools.partial
    vectors = ((pairs, half, width), BF16)
    edges = ((2, half, width), BF16)
    forward_shape = ((6, pairs, half, width), F32)
    backward_shape = ((8, pairs, half, width), F32)
    blocks = ((cells, width, width), BF16)
    packed_shape = ((cells + 1, half, width), F32)

    source, packed = run(
        pack_kernel, [packed_shape, packed_shape], rhs, span_link, hbm=(0, 1),
        scratch=[pltpu.VMEM((1, cells), jnp.int32)] + [pltpu.SemaphoreType.DMA] * 3,
    )
    lower_x = swapped(lower_up)
    source_x = swapped(packed)
    side_x = swapped(after(lower_span, source_x))
    rows = (source, source_x)
    lowers = (lower_up, lower_x)
    sides = (lower_span, side_x)
    state, out = run(first_kernel, [forward_shape, vectors], *rows, *lowers)
    even_recv = hop(out, 0, 1)
    state, heads = run(first_heads_kernel, [forward_shape, edges], state, alias={0: 0})
    heads = beside(heads, 0, -1)
    both, chain = run(ahead_kernel, [blocks, blocks], *lowers, dinv, upper_down)

    for turn in range(last + 1):
        if turn > 0:
            state, out = run(
                part(even_kernel, turn), [forward_shape, vectors], even_recv, both, state,
                alias={2: 0},
            )
            here = even_recv
            if turn < last:
                even_recv = hop(out, turn, turn + 1)
            state, heads = run(
                part(heads_kernel, turn), [forward_shape, edges], here, *lowers, state,
                alias={3: 0},
            )
            heads = beside(heads, turn, -1)
        else:
            here = out
        (state,) = run(
            part(odd_source_kernel, turn), [forward_shape], here, *rows, *lowers, *sides, state,
            alias={7: 0},
        )
        (state,) = run(
            part(odd_last_kernel, turn), [forward_shape], heads, *rows, *lowers, *sides, state,
            alias={7: 0},
        )
        if turn == 0:
            state, out = run(first_odd_kernel, [forward_shape, vectors], state, alias={0: 0})
        else:
            state, out = run(
                part(odd_kernel, turn), [forward_shape, vectors], odd_recv, both, state,
                alias={2: 0},
            )
        if turn < last:
            odd_recv = hop(out, turn, turn + 1)
        if turn == 3:
            (chain,) = run(chain_kernel, [blocks], dinv, upper_down, state, chain, alias={3: 0})
            chain_x = swapped(chain)
        if turn == 4:
            inverse_x = swapped(after(dinv, state))
        if turn == 5:
            above_x = swapped(after(upper_span, state))

    forward = state
    chains = (chain, chain_x)
    inverses = (dinv, inverse_x)
    aboves = (upper_span, above_x)
    state, out = run(
        turn_back_kernel, [backward_shape, vectors], forward, *lowers, *inverses, *chains
    )
    odd_recv = hop(out, last, last - 1)
    state, tails = run(first_tails_kernel, [backward_shape, edges], *rows, state, alias={2: 0})
    tails = beside(tails, last, 1)
    (both,) = run(part(back_product_kernel, last), [blocks], *chains)

    for turn in range(last + 1):
        stage = last - turn
        if turn > 0:
            state, out = run(
                part(odd_low_kernel, stage), [backward_shape, vectors], odd_recv, both, state,
                alias={2: 0},
            )
            here = odd_recv
            if turn < last:
                odd_recv = hop(out, stage, stage - 1)
            state, tails = run(
                part(tails_kernel, stage), [backward_shape, edges], here, *rows, *chains, state,
                alias={5: 0},
            )
            tails = beside(tails, stage, 1)
        else:
            here = out
        (state,) = run(
            part(even_gain_kernel, stage, turn == 0), [backward_shape], here, *rows, forward,
            *aboves, *inverses, *chains, state, alias={10: 0},
        )
        (state,) = run(
            part(even_first_kernel, stage), [backward_shape], tails, *aboves, *inverses,
            *chains, state, alias={7: 0},
        )
        if turn == 0:
            state, out = run(
                first_even_out_kernel, [backward_shape, vectors], state, alias={0: 0}
            )
        else:
            state, out = run(
                part(even_out_kernel, stage), [backward_shape, vectors], even_recv, both, state,
                alias={2: 0},
            )
        if turn < last:
            even_recv = hop(out, stage, stage - 1)

    kept, sent = run(
        split_kernel, [((cells, half, width), F32), ((cells, half, width), BF16)], state, *chains
    )
    arrived = swapped(sent)
    in_vmem = pl.BlockSpec(memory_space=pltpu.VMEM)
    result = pl.pallas_call(
        join_kernel,
        out_shape=jax.ShapeDtypeStruct((cells, vecs, width), F32),
        in_specs=[in_vmem] * 2,
        out_specs=in_vmem,
        compiler_params=pltpu.CompilerParams(vmem_limit_bytes=LIMIT),
    )(kept, arrived)
    return result[None]


def solution(mesh):
    return jax.shard_map(
        shards,
        mesh=mesh,
        in_specs=(
            P("stream", "span", None, None),
            P("stream", "span", None, None),
            P("stream", "span", None, None),
            P("stream", "span", None, None, None),
            P("stream", "span", None, None),
            P("stream", "span", None, None, None),
            P("stream", "span"),
        ),
        out_specs=P("stream", "span", None, None),
        check_vma=False,
    )
```

```python
import functools
import jax
import jax.numpy as jnp
from jax import lax
from jax.experimental import pallas as pl
from jax.experimental.pallas import tpu as pltpu
from jax.sharding import PartitionSpec as P

F32 = jnp.float32
BF16 = jnp.bfloat16
LIMIT = 10 * 1024 * 1024
LOAD_LIMIT = 59 * 1024 * 1024
SPAN_PERIOD = 4
GATHER_TURN = 3
CHAIN, INVERSE, SIDE = range(3)

EVEN_LOW, EVEN_HIGH, ODD_LOW, ODD_HIGH, ODD_PART, ODD_INFLOW = range(6)
REST_LOW, REST_HIGH, OUT_ODD_LOW, OUT_ODD_HIGH, GAIN_LOW, GAIN_HIGH, OUT_EVEN_LOW, EVEN_INFLOW = range(8)


def times(vectors, block):
    return lax.dot_general(
        vectors.astype(BF16), block, (((1,), (1,)), ((), ())), preferred_element_type=F32
    )


def product(left, right):
    return lax.dot_general(left, right, (((1,), (0,)), ((), ())), preferred_element_type=F32)


def run(body, outs, *operands, alias=None, hbm=(), scratch=(), limit=LIMIT):
    in_vmem = pl.BlockSpec(memory_space=pltpu.VMEM)
    in_hbm = pl.BlockSpec(memory_space=pltpu.HBM)
    return pl.pallas_call(
        body,
        out_shape=[pltpu.VMEM(shape, dtype) for shape, dtype in outs],
        in_specs=[in_hbm if index in hbm else in_vmem for index in range(len(operands))],
        out_specs=[in_vmem] * len(outs),
        input_output_aliases=alias or {},
        scratch_shapes=list(scratch),
        compiler_params=pltpu.CompilerParams(vmem_limit_bytes=limit),
    )(*operands)


def place():
    stream = lax.axis_index("stream")
    return stream // 2, stream % 2


def ordered(active, core, own, other, work):
    @pl.when(active & (core == 0))
    def _():
        work(own, other)

    @pl.when(active & (core == 1))
    def _():
        work(other, own)


def half_rows(core, half):
    return pl.ds(pl.multiple_of(core * half, half), half)


def load_kernel(rhs, lower, own, sent, even, odd, *sems):
    _, core = place()
    half = own.shape[1]
    copies = [
        (rhs.at[:, half_rows(1 - core, half), :], sent),
        (lower.at[:, 0], even),
        (lower.at[:, 1], odd),
        (rhs.at[:, half_rows(core, half), :], own),
    ]
    copies = [pltpu.make_async_copy(*ends, sem) for ends, sem in zip(copies, sems)]
    for copy in copies:
        copy.start()
    for copy in copies:
        copy.wait()


def first_kernel(source, source_x, lower, lower_x, state, out):
    _, core = place()
    pairs = out.shape[0]

    def work(low, high):
        for pair in range(pairs):
            fresh = high[0][2 * pair] - times(low[0][2 * pair], high[1][pair])
            out[pair] = fresh.astype(BF16)
            state[EVEN_HIGH, pair] = fresh
        for pair in range(pairs):
            state[EVEN_LOW, pair] = low[0][2 * pair]

    ordered(True, core, (source, lower), (source_x, lower_x), work)


def ahead_kernel(lower, lower_x, both):
    stage, core = place()

    def work(low, high):
        for pair in range(both.shape[0]):
            both[pair] = product(high[pair], low[pair]).astype(BF16)

    ordered(stage > 0, core, lower, lower_x, work)


def gather_back(inverse, upper, side, packed, upper_here, sems):
    copies = [
        pltpu.make_async_copy(upper, upper_here, sems[0]),
        pltpu.make_async_copy(inverse, packed.at[INVERSE], sems[1]),
        pltpu.make_async_copy(side, packed.at[SIDE], sems[2]),
    ]
    for copy in copies:
        copy.start()
    for copy in copies:
        copy.wait()
    for cell in range(packed.shape[1]):
        packed[CHAIN, cell] = product(packed[INVERSE, cell], upper_here[cell]).astype(BF16)


def gather_early_kernel(
    even, even_x, inverse, upper, side, both, packed, upper_here, *sems
):
    stage, _ = place()
    ahead_kernel(even, even_x, both)

    @pl.when(stage >= GATHER_TURN)
    def _():
        gather_back(inverse, upper, side, packed, upper_here, sems)


def even_kernel(turn, recv, both, state_in, state, out):
    stage, _ = place()

    @pl.when(stage == turn)
    def _():
        for pair in range(out.shape[0]):
            fresh = state[EVEN_HIGH, pair] + times(recv[pair], both[pair])
            out[pair] = fresh.astype(BF16)
            state[EVEN_HIGH, pair] = fresh


def even_gather_kernel(
    recv, both, inverse, upper, side, state_in, packed_in, state, out, packed, upper_here, *sems
):
    stage, _ = place()
    even_kernel(GATHER_TURN, recv, both, state_in, state, out)

    @pl.when(stage < GATHER_TURN)
    def _():
        gather_back(inverse, upper, side, packed, upper_here, sems)


def back_product_kernel(last, packed, packed_x, both_even, both_odd):
    stage, core = place()

    def work(low, high):
        for parity, both in enumerate((both_even, both_odd)):
            for pair in range(both.shape[0]):
                cell = 2 * pair + parity
                both[pair] = product(low[CHAIN, cell], high[CHAIN, cell]).astype(BF16)

    ordered(stage < last, core, packed, packed_x, work)


def heads_kernel(turn, recv, lower, lower_x, state_in, state, heads):
    stage, core = place()

    def work(low, high):
        state[EVEN_LOW, 0] = state[EVEN_LOW, 0] - times(recv[0], low[0])
        heads[0] = state[EVEN_LOW, 0].astype(BF16)
        heads[1] = state[EVEN_HIGH, 0].astype(BF16)

    ordered(stage == turn, core, lower, lower_x, work)


def first_heads_kernel(state_in, state, heads):
    heads[0] = state[EVEN_LOW, 0].astype(BF16)
    heads[1] = state[EVEN_HIGH, 0].astype(BF16)


def link_of(link, cell):
    return link[0:1, cell : cell + 1].astype(F32)


def odd_source_kernel(
    turn, recv, source, source_x, link, link_x, even, even_x, odd, odd_x, side, side_x,
    state_in, state
):
    stage, core = place()
    pairs = side.shape[0]

    def work(low, high):
        if turn > 0:
            for pair in range(1, pairs):
                state[EVEN_LOW, pair] = state[EVEN_LOW, pair] - times(recv[pair], low[1][pair])
        for layer, (values, _, _, sides, links) in enumerate((low, high)):
            near, row = ((EVEN_LOW, ODD_LOW), (EVEN_HIGH, ODD_PART))[layer]
            for pair in range(pairs):
                fresh = values[2 * pair + 1]
                fresh = fresh - link_of(links, 2 * pair) * times(
                    state[near, pair], sides[pair, 0]
                )
                if pair + 1 < pairs:
                    fresh = fresh - link_of(links, 2 * pair + 1) * times(
                        state[near, pair + 1], sides[pair, 1]
                    )
                state[row, pair] = fresh
        for pair in range(pairs - 1):
            state[ODD_PART, pair] = state[ODD_PART, pair] - times(
                state[ODD_LOW, pair], high[2][pair]
            )

    ordered(
        stage == turn, core,
        (source, even, odd, side, link), (source_x, even_x, odd_x, side_x, link_x), work,
    )


def odd_last_kernel(turn, heads, link, link_x, odd, odd_x, side, side_x, state_in, state):
    stage, core = place()
    pair = side.shape[0] - 1

    def work(low, high):
        for layer, (links, _, sides) in enumerate((low, high)):
            row = (ODD_LOW, ODD_PART)[layer]
            state[row, pair] = state[row, pair] - link_of(links, 2 * pair + 1) * times(
                heads[layer], sides[pair, 1]
            )
        state[ODD_PART, pair] = state[ODD_PART, pair] - times(
            state[ODD_LOW, pair], high[1][pair]
        )

    ordered(stage == turn, core, (link, odd, side), (link_x, odd_x, side_x), work)


def odd_kernel(turn, recv, both, state_in, state, out):
    stage, _ = place()

    @pl.when(stage == turn)
    def _():
        for pair in range(out.shape[0]):
            fresh = state[ODD_PART, pair] + times(recv[pair], both[pair])
            out[pair] = fresh.astype(BF16)
            state[ODD_HIGH, pair] = fresh
            state[ODD_INFLOW, pair] = recv[pair].astype(F32)


def first_odd_kernel(state_in, state, out):
    for pair in range(out.shape[0]):
        fresh = state[ODD_PART, pair]
        out[pair] = fresh.astype(BF16)
        state[ODD_HIGH, pair] = fresh
        state[ODD_INFLOW, pair] = jnp.zeros(fresh.shape, F32)


def turn_back_kernel(forward, lower, lower_x, packed, packed_x, state, out):
    _, core = place()
    pairs = out.shape[0]

    def work(low, high):
        for pair in range(pairs):
            cell = 2 * pair + 1
            high_rest = times(forward[ODD_HIGH, pair], high[1][INVERSE, cell])
            low_value = forward[ODD_LOW, pair] - times(forward[ODD_INFLOW, pair], low[0][pair])
            low_rest = times(low_value, low[1][INVERSE, cell])
            low_rest = low_rest - times(high_rest, low[1][CHAIN, cell])
            state[REST_HIGH, pair] = high_rest
            state[OUT_ODD_HIGH, pair] = high_rest
            state[REST_LOW, pair] = low_rest
            state[OUT_ODD_LOW, pair] = low_rest
            out[pair] = low_rest.astype(BF16)

    ordered(True, core, (lower, packed), (lower_x, packed_x), work)


def odd_low_kernel(stage_of_turn, recv, both, state_in, state, out):
    stage, _ = place()

    @pl.when(stage == stage_of_turn)
    def _():
        for pair in range(out.shape[0]):
            fresh = state[REST_LOW, pair] + times(recv[pair], both[pair])
            out[pair] = fresh.astype(BF16)
            state[OUT_ODD_LOW, pair] = fresh


def even_out_kernel(stage_of_turn, recv, both, state_in, state, out):
    stage, _ = place()

    @pl.when(stage == stage_of_turn)
    def _():
        for pair in range(out.shape[0]):
            fresh = state[GAIN_LOW, pair] + times(recv[pair], both[pair])
            out[pair] = fresh.astype(BF16)
            state[OUT_EVEN_LOW, pair] = fresh
            state[EVEN_INFLOW, pair] = recv[pair].astype(F32)


def first_even_out_kernel(state_in, state, out):
    for pair in range(out.shape[0]):
        fresh = state[GAIN_LOW, pair]
        out[pair] = fresh.astype(BF16)
        state[OUT_EVEN_LOW, pair] = fresh
        state[EVEN_INFLOW, pair] = jnp.zeros(fresh.shape, F32)


def tails_of(low, high, state, tails):
    pairs = state.shape[1]
    for layer, (links, row) in enumerate(((low, OUT_ODD_LOW), (high, OUT_ODD_HIGH))):
        tails[layer] = (state[row, pairs - 1] * link_of(links, 2 * pairs - 1)).astype(BF16)


def tails_kernel(stage_of_turn, recv, link, link_x, packed, packed_x, state_in, state, tails):
    stage, core = place()
    pair = recv.shape[0] - 1

    def work(low, high):
        state[OUT_ODD_HIGH, pair] = state[REST_HIGH, pair] - times(
            recv[pair], high[1][CHAIN, 2 * pair + 1]
        )
        tails_of(low[0], high[0], state, tails)

    ordered(stage == stage_of_turn, core, (link, packed), (link_x, packed_x), work)


def first_tails_kernel(link, link_x, state_in, state, tails):
    _, core = place()
    ordered(True, core, link, link_x, lambda low, high: tails_of(low, high, state, tails))


def settle_gain(state, low, high, pair):
    high_gain = times(state[GAIN_HIGH, pair], high[INVERSE, 2 * pair])
    low_gain = times(state[GAIN_LOW, pair], low[INVERSE, 2 * pair])
    state[GAIN_HIGH, pair] = high_gain
    state[GAIN_LOW, pair] = low_gain - times(high_gain, low[CHAIN, 2 * pair])


def even_gain_kernel(
    stage_of_turn, first, recv, link, link_x, forward, packed, packed_x, state_in, state
):
    stage, core = place()
    pairs = recv.shape[0]

    def work(low, high):
        if not first:
            for pair in range(pairs - 1):
                state[OUT_ODD_HIGH, pair] = state[REST_HIGH, pair] - times(
                    recv[pair], high[0][CHAIN, 2 * pair + 1]
                )
        for layer, (blocks, links) in enumerate((low, high)):
            near, odd, gain = (
                (EVEN_LOW, OUT_ODD_LOW, GAIN_LOW),
                (EVEN_HIGH, OUT_ODD_HIGH, GAIN_HIGH),
            )[layer]
            for pair in range(pairs):
                fresh = forward[near, pair]
                if pair > 0:
                    fresh = fresh - link_of(links, 2 * pair - 1) * times(
                        state[odd, pair - 1], blocks[SIDE, 2 * pair]
                    )
                fresh = fresh - link_of(links, 2 * pair) * times(
                    state[odd, pair], blocks[SIDE, 2 * pair + 1]
                )
                state[gain, pair] = fresh
        for pair in range(1, pairs):
            settle_gain(state, low[0], high[0], pair)

    ordered(stage == stage_of_turn, core, (packed, link), (packed_x, link_x), work)


def even_first_kernel(stage_of_turn, tails, packed, packed_x, state_in, state):
    stage, core = place()

    def work(low, high):
        for layer, blocks in enumerate((low, high)):
            gain = (GAIN_LOW, GAIN_HIGH)[layer]
            state[gain, 0] = state[gain, 0] - times(tails[layer], blocks[SIDE, 0])
        settle_gain(state, low, high, 0)

    ordered(stage == stage_of_turn, core, packed, packed_x, work)


def split_kernel(state, packed, packed_x, kept, sent):
    _, core = place()
    pairs = state.shape[1]

    def work(low, high):
        for pair in range(pairs):
            even_high = state[GAIN_HIGH, pair] - times(
                state[EVEN_INFLOW, pair], high[CHAIN, 2 * pair]
            )
            if low is packed:
                kept[2 * pair] = state[OUT_EVEN_LOW, pair]
                kept[2 * pair + 1] = state[OUT_ODD_LOW, pair]
                sent[2 * pair] = even_high.astype(BF16)
                sent[2 * pair + 1] = state[OUT_ODD_HIGH, pair].astype(BF16)
            else:
                sent[2 * pair] = state[OUT_EVEN_LOW, pair].astype(BF16)
                sent[2 * pair + 1] = state[OUT_ODD_LOW, pair].astype(BF16)
                kept[2 * pair] = even_high
                kept[2 * pair + 1] = state[OUT_ODD_HIGH, pair]

    ordered(True, core, packed, packed_x, work)


def join_kernel(kept, arrived, result):
    _, core = place()
    cells, half = kept.shape[0], kept.shape[1]
    for cell in range(cells):
        result[cell, half_rows(core, half), :] = kept[cell]
        result[cell, half_rows(1 - core, half), :] = arrived[cell].astype(F32)


def shards(rhs, dinv, lower_up, lower_span, upper_down, upper_span, span_link):
    rhs, dinv, lower_up = rhs[0], dinv[0], lower_up[0]
    lower_span, upper_down, upper_span = lower_span[0], upper_down[0], upper_span[0]
    cells, vecs, width = rhs.shape
    pairs, half = cells // 2, vecs // 2
    streams, spans = lax.axis_size("stream"), lax.axis_size("span")
    last = streams // 2 - 1

    def swapped(value):
        return lax.ppermute(value, "stream", [(index, index ^ 1) for index in range(streams)])

    def hop(value, start, end):
        return lax.ppermute(
            value, "stream", [(2 * start + core, 2 * end + core) for core in (0, 1)]
        )

    def beside(value, stage, step):
        links = []
        for member in range(stage % SPAN_PERIOD, last + 1, SPAN_PERIOD):
            for core in (0, 1):
                for span in range(spans):
                    if 0 <= span + step < spans:
                        base = (2 * member + core) * spans + span
                        links.append((base, base + step))
        return lax.ppermute(value, ("stream", "span"), links)

    def after(value, *others):
        return lax.optimization_barrier((value,) + others)[0]

    part = functools.partial
    vectors = ((pairs, half, width), BF16)
    edges = ((2, half, width), BF16)
    forward_shape = ((6, pairs, half, width), F32)
    backward_shape = ((8, pairs, half, width), F32)
    blocks = ((cells, width, width), BF16)
    packed_shape = ((cells, half, width), F32)
    lower_shape = ((pairs, width, width), BF16)

    source, packed, lower_even, lower_odd = run(
        load_kernel, [packed_shape, packed_shape, lower_shape, lower_shape],
        rhs, lower_up.reshape(pairs, 2, width, width), hbm=(0, 1),
        scratch=[pltpu.SemaphoreType.DMA] * 4, limit=LOAD_LIMIT,
    )
    source_x = swapped(packed)
    lower_even_x = swapped(lower_even)
    lower_odd_x = swapped(after(lower_odd, source_x))
    side_x = swapped(after(lower_span, lower_even_x, source_x))
    link_x = swapped(after(span_link, lower_even_x))
    rows = (source, source_x)
    links = (span_link, link_x)
    evens = (lower_even, lower_even_x)
    odds = (lower_odd, lower_odd_x)
    sides = (lower_span, side_x)

    def even_turn(turn, recv, state):
        if turn == GATHER_TURN:
            state, out, packed = run(
                even_gather_kernel, [forward_shape, vectors, packed_shape], recv, both_even,
                *backs, state, early, alias={5: 0, 6: 2}, hbm=(2, 3, 4), **gathering,
            )
            packs.extend((packed, swapped(packed)))
        else:
            state, out = run(
                part(even_kernel, turn), [forward_shape, vectors], recv, both_even, state,
                alias={2: 0},
            )
        sent = hop(out, turn, turn + 1) if turn < last else None
        state, heads = run(
            part(heads_kernel, turn), [forward_shape, edges], recv, *evens, state, alias={3: 0}
        )
        return state, sent, beside(heads, turn, -1)

    def odd_ready(turn, recv, heads, state):
        (state,) = run(
            part(odd_source_kernel, turn), [forward_shape], recv, *rows, *links, *evens, *odds,
            *sides, state, alias={11: 0},
        )
        (state,) = run(
            part(odd_last_kernel, turn), [forward_shape], heads, *links, *odds, *sides, state,
            alias={7: 0},
        )
        return state

    def odd_turn(turn, recv, state):
        state, out = run(
            part(odd_kernel, turn), [forward_shape, vectors], recv, both_odd, state, alias={2: 0}
        )
        return state, hop(out, turn, turn + 1) if turn < last else None

    backs = (dinv, upper_down, upper_span.reshape(cells, width, width))
    gathering = dict(
        scratch=[pltpu.VMEM((cells, width, width), BF16)] + [pltpu.SemaphoreType.DMA] * 3
    )
    packed_shape = ((3, cells, width, width), BF16)
    packs = []

    state, out = run(first_kernel, [forward_shape, vectors], *rows, *evens)
    even_recv = hop(out, 0, 1)
    state, heads = run(first_heads_kernel, [forward_shape, edges], state, alias={0: 0})
    heads = beside(heads, 0, -1)
    both_even, early = run(
        gather_early_kernel, [lower_shape, packed_shape], *evens, *backs, hbm=(2, 3, 4),
        **gathering,
    )
    state = odd_ready(0, out, heads, after(state, both_even))
    state, out = run(first_odd_kernel, [forward_shape, vectors], state, alias={0: 0})
    odd_recv = hop(out, 0, 1)
    here = even_recv
    state, even_recv, heads = even_turn(1, here, state)
    (both_odd,) = run(ahead_kernel, [lower_shape], after(lower_odd, state), lower_odd_x)
    state = odd_ready(1, here, heads, after(state, both_odd))
    state, odd_recv = odd_turn(1, odd_recv, state)
    for turn in range(2, last):
        here = even_recv
        state, even_recv, heads = even_turn(turn, here, state)
        state = odd_ready(turn, here, heads, state)
        if turn == last - 1:
            here = even_recv
            state, _, heads = even_turn(last, here, state)
        state, odd_recv = odd_turn(turn, odd_recv, state)
    state = odd_ready(last, here, heads, state)
    forward, _ = odd_turn(last, odd_recv, state)

    def back_odd_turn(stage, recv, state):
        state, out = run(
            part(odd_low_kernel, stage), [backward_shape, vectors], recv, both_odd, state,
            alias={2: 0},
        )
        sent = hop(out, stage, stage - 1) if stage > 0 else None
        state, tails = run(
            part(tails_kernel, stage), [backward_shape, edges], recv, *links, *packs, state,
            alias={5: 0},
        )
        return state, sent, beside(tails, stage, 1)

    def even_ready(stage, recv, tails, state):
        (state,) = run(
            part(even_gain_kernel, stage, stage == last), [backward_shape], recv, *links, forward,
            *packs, state, alias={6: 0},
        )
        (state,) = run(
            part(even_first_kernel, stage), [backward_shape], tails, *packs, state, alias={3: 0}
        )
        return state

    def back_even_turn(stage, recv, state):
        state, out = run(
            part(even_out_kernel, stage), [backward_shape, vectors], recv, both_even, state,
            alias={2: 0},
        )
        return state, hop(out, stage, stage - 1) if stage > 0 else None

    state, out = run(turn_back_kernel, [backward_shape, vectors], forward, *odds, *packs)
    odd_recv = hop(out, last, last - 1)
    state, tails = run(first_tails_kernel, [backward_shape, edges], *links, state, alias={2: 0})
    tails = beside(tails, last, 1)
    both_even, both_odd = run(part(back_product_kernel, last), [lower_shape] * 2, *packs)
    state = even_ready(last, out, tails, after(state, both_odd))
    state, out = run(first_even_out_kernel, [backward_shape, vectors], state, alias={0: 0})
    even_recv = hop(out, last, last - 1)
    for stage in range(last - 1, 0, -1):
        here = odd_recv
        state, odd_recv, tails = back_odd_turn(stage, here, state)
        state = even_ready(stage, here, tails, state)
        if stage == 1:
            here = odd_recv
            state, _, tails = back_odd_turn(0, here, state)
        state, even_recv = back_even_turn(stage, even_recv, state)
    state = even_ready(0, here, tails, state)
    state, _ = back_even_turn(0, even_recv, state)

    kept, sent = run(
        split_kernel, [((cells, half, width), F32), ((cells, half, width), BF16)], state, *packs
    )
    arrived = swapped(sent)
    in_vmem = pl.BlockSpec(memory_space=pltpu.VMEM)
    result = pl.pallas_call(
        join_kernel,
        out_shape=jax.ShapeDtypeStruct((cells, vecs, width), F32),
        in_specs=[in_vmem] * 2,
        out_specs=in_vmem,
        compiler_params=pltpu.CompilerParams(vmem_limit_bytes=LIMIT),
    )(kept, arrived)
    return result[None]


def solution(mesh):
    return jax.shard_map(
        shards,
        mesh=mesh,
        in_specs=(
            P("stream", "span", None, None),
            P("stream", "span", None, None),
            P("stream", "span", None, None),
            P("stream", "span", None, None, None),
            P("stream", "span", None, None),
            P("stream", "span", None, None, None),
            P("stream", "span"),
        ),
        out_specs=P("stream", "span", None, None),
        check_vma=False,
    )
```

```python
import functools
import jax
import jax.numpy as jnp
from jax import lax
from jax.experimental import pallas as pl
from jax.experimental.pallas import tpu as pltpu
from jax.sharding import PartitionSpec as P

F32 = jnp.float32
BF16 = jnp.bfloat16
LIMIT = 10 * 1024 * 1024
SPAN_PERIOD = 4
GATHER_TURN = 4
GATHER_FROM = 3
CHAIN, INVERSE, SIDE = range(3)

EVEN_LOW, EVEN_HIGH, ODD_LOW, ODD_HIGH, ODD_PART, ODD_INFLOW = range(6)
REST_LOW, REST_HIGH, OUT_ODD_LOW, OUT_ODD_HIGH, GAIN_LOW, GAIN_HIGH, OUT_EVEN_LOW, EVEN_INFLOW = range(8)


def times(vectors, block):
    return lax.dot_general(
        vectors.astype(BF16), block, (((1,), (1,)), ((), ())), preferred_element_type=F32
    )


def product(left, right):
    return lax.dot_general(left, right, (((1,), (0,)), ((), ())), preferred_element_type=F32)


def turned_product(left, right):
    return lax.dot_general(right, left, (((0,), (1,)), ((), ())), preferred_element_type=F32)


def times_turned(vectors, block):
    return product(vectors.astype(BF16), block)


def run(body, outs, *operands, alias=None, hbm=(), scratch=()):
    in_vmem = pl.BlockSpec(memory_space=pltpu.VMEM)
    in_hbm = pl.BlockSpec(memory_space=pltpu.HBM)
    return pl.pallas_call(
        body,
        out_shape=[pltpu.VMEM(shape, dtype) for shape, dtype in outs],
        in_specs=[in_hbm if index in hbm else in_vmem for index in range(len(operands))],
        out_specs=[in_vmem] * len(outs),
        input_output_aliases=alias or {},
        scratch_shapes=list(scratch),
        compiler_params=pltpu.CompilerParams(vmem_limit_bytes=LIMIT),
    )(*operands)


def place():
    stream = lax.axis_index("stream")
    return stream // 2, stream % 2


def ordered(active, core, own, other, work):
    @pl.when(active & (core == 0))
    def _():
        work(own, other)

    @pl.when(active & (core == 1))
    def _():
        work(other, own)


def half_rows(core, half):
    return pl.ds(pl.multiple_of(core * half, half), half)


def load_kernel(rhs, lower, own, sent, even, odd, *sems):
    _, core = place()
    half = own.shape[1]
    copies = [
        (rhs.at[:, half_rows(1 - core, half), :], sent),
        (lower.at[:, 0], even),
        (lower.at[:, 1], odd),
        (rhs.at[:, half_rows(core, half), :], own),
    ]
    copies = [pltpu.make_async_copy(*ends, sem) for ends, sem in zip(copies, sems)]
    for copy in copies:
        copy.start()
    for copy in copies:
        copy.wait()


def first_kernel(source, source_x, lower, lower_x, state, out):
    _, core = place()
    pairs = out.shape[0]

    def work(low, high):
        for pair in range(pairs):
            fresh = high[0][2 * pair] - times(low[0][2 * pair], high[1][pair])
            out[pair] = fresh.astype(BF16)
            state[EVEN_HIGH, pair] = fresh
        for pair in range(pairs):
            state[EVEN_LOW, pair] = low[0][2 * pair]

    ordered(True, core, (source, lower), (source_x, lower_x), work)


def ahead_kernel(lower, lower_x, both):
    stage, core = place()

    def work(low, high):
        for pair in range(both.shape[0]):
            both[pair] = turned_product(high[pair], low[pair]).astype(BF16)

    ordered(stage > 0, core, lower, lower_x, work)


def gather_back(inverse, upper, side, packed, upper_here, sems):
    copies = [
        pltpu.make_async_copy(upper, upper_here, sems[0]),
        pltpu.make_async_copy(inverse, packed.at[INVERSE], sems[1]),
        pltpu.make_async_copy(side, packed.at[SIDE], sems[2]),
    ]
    for copy in copies:
        copy.start()
    for copy in copies:
        copy.wait()
    for cell in range(packed.shape[1]):
        packed[CHAIN, cell] = turned_product(packed[INVERSE, cell], upper_here[cell]).astype(BF16)


def gather_early_kernel(
    even, even_x, inverse, upper, side, both, packed, upper_here, *sems
):
    stage, _ = place()
    ahead_kernel(even, even_x, both)

    @pl.when(stage >= GATHER_FROM)
    def _():
        gather_back(inverse, upper, side, packed, upper_here, sems)


def even_kernel(turn, recv, both, state_in, state, out=None):
    stage, _ = place()

    @pl.when(stage == turn)
    def _():
        for pair in range(recv.shape[0]):
            fresh = state[EVEN_HIGH, pair] + times_turned(recv[pair], both[pair])
            if out is not None:
                out[pair] = fresh.astype(BF16)
            state[EVEN_HIGH, pair] = fresh


def back_product_kernel(last, packed, packed_x, both_even, both_odd):
    stage, core = place()

    def work(low, high):
        for parity, both in enumerate((both_even, both_odd)):
            for pair in range(both.shape[0]):
                cell = 2 * pair + parity
                both[pair] = product(high[CHAIN, cell], low[CHAIN, cell]).astype(BF16)

    ordered(stage < last, core, packed, packed_x, work)


def even_gather_kernel(
    recv, both, inverse, upper, side, state_in, packed_in, state, out, packed, upper_here, *sems
):
    stage, _ = place()
    even_kernel(GATHER_TURN, recv, both, state_in, state, out)

    @pl.when(stage < GATHER_FROM)
    def _():
        gather_back(inverse, upper, side, packed, upper_here, sems)


def heads_kernel(turn, recv, lower, lower_x, state_in, state, heads):
    stage, core = place()

    def work(low, high):
        state[EVEN_LOW, 0] = state[EVEN_LOW, 0] - times(recv[0], low[0])
        heads[0] = state[EVEN_LOW, 0].astype(BF16)
        heads[1] = state[EVEN_HIGH, 0].astype(BF16)

    ordered(stage == turn, core, lower, lower_x, work)


def first_heads_kernel(state_in, state, heads):
    heads[0] = state[EVEN_LOW, 0].astype(BF16)
    heads[1] = state[EVEN_HIGH, 0].astype(BF16)


def link_of(link, cell):
    return link[0:1, cell : cell + 1].astype(F32)


def odd_source_kernel(
    turn, recv, source, source_x, link, link_x, even, even_x, odd, odd_x, side, side_x,
    state_in, state
):
    stage, core = place()
    pairs = side.shape[0]

    def work(low, high):
        if turn > 0:
            for pair in range(1, pairs):
                state[EVEN_LOW, pair] = state[EVEN_LOW, pair] - times(recv[pair], low[1][pair])
        for layer, (values, _, _, sides, links) in enumerate((low, high)):
            near, row = ((EVEN_LOW, ODD_LOW), (EVEN_HIGH, ODD_PART))[layer]
            for pair in range(pairs):
                fresh = values[2 * pair + 1]
                fresh = fresh - link_of(links, 2 * pair) * times(
                    state[near, pair], sides[pair, 0]
                )
                if pair + 1 < pairs:
                    fresh = fresh - link_of(links, 2 * pair + 1) * times(
                        state[near, pair + 1], sides[pair, 1]
                    )
                state[row, pair] = fresh
        for pair in range(pairs - 1):
            state[ODD_PART, pair] = state[ODD_PART, pair] - times(
                state[ODD_LOW, pair], high[2][pair]
            )

    ordered(
        stage == turn, core,
        (source, even, odd, side, link), (source_x, even_x, odd_x, side_x, link_x), work,
    )


def odd_last_kernel(turn, heads, link, link_x, odd, odd_x, side, side_x, state_in, state):
    stage, core = place()
    pair = side.shape[0] - 1

    def work(low, high):
        for layer, (links, _, sides) in enumerate((low, high)):
            row = (ODD_LOW, ODD_PART)[layer]
            state[row, pair] = state[row, pair] - link_of(links, 2 * pair + 1) * times(
                heads[layer], sides[pair, 1]
            )
        state[ODD_PART, pair] = state[ODD_PART, pair] - times(
            state[ODD_LOW, pair], high[1][pair]
        )

    ordered(stage == turn, core, (link, odd, side), (link_x, odd_x, side_x), work)


def odd_kernel(turn, recv, both, state_in, state, out=None):
    stage, _ = place()

    @pl.when(stage == turn)
    def _():
        for pair in range(recv.shape[0]):
            fresh = state[ODD_PART, pair] + times_turned(recv[pair], both[pair])
            if out is not None:
                out[pair] = fresh.astype(BF16)
            state[ODD_HIGH, pair] = fresh
            state[ODD_INFLOW, pair] = recv[pair].astype(F32)


def first_odd_kernel(state_in, state, out):
    for pair in range(out.shape[0]):
        fresh = state[ODD_PART, pair]
        out[pair] = fresh.astype(BF16)
        state[ODD_HIGH, pair] = fresh
        state[ODD_INFLOW, pair] = jnp.zeros(fresh.shape, F32)


def turn_back_kernel(forward, lower, lower_x, packed, packed_x, state, out):
    _, core = place()
    pairs = out.shape[0]

    def work(low, high):
        for pair in range(pairs):
            cell = 2 * pair + 1
            high_rest = times(forward[ODD_HIGH, pair], high[1][INVERSE, cell])
            low_value = forward[ODD_LOW, pair] - times(forward[ODD_INFLOW, pair], low[0][pair])
            low_rest = times(low_value, low[1][INVERSE, cell])
            low_rest = low_rest - times_turned(high_rest, low[1][CHAIN, cell])
            state[REST_HIGH, pair] = high_rest
            state[OUT_ODD_HIGH, pair] = high_rest
            state[REST_LOW, pair] = low_rest
            state[OUT_ODD_LOW, pair] = low_rest
            out[pair] = low_rest.astype(BF16)

    ordered(True, core, (lower, packed), (lower_x, packed_x), work)


def odd_low_kernel(stage_of_turn, recv, both, state_in, state, out=None):
    stage, _ = place()

    @pl.when(stage == stage_of_turn)
    def _():
        for pair in range(recv.shape[0]):
            fresh = state[REST_LOW, pair] + times_turned(recv[pair], both[pair])
            if out is not None:
                out[pair] = fresh.astype(BF16)
            state[OUT_ODD_LOW, pair] = fresh


def even_out_kernel(stage_of_turn, recv, both, state_in, state, out=None):
    stage, _ = place()

    @pl.when(stage == stage_of_turn)
    def _():
        for pair in range(recv.shape[0]):
            fresh = state[GAIN_LOW, pair] + times_turned(recv[pair], both[pair])
            if out is not None:
                out[pair] = fresh.astype(BF16)
            state[OUT_EVEN_LOW, pair] = fresh
            state[EVEN_INFLOW, pair] = recv[pair].astype(F32)


def first_even_out_kernel(state_in, state, out):
    for pair in range(out.shape[0]):
        fresh = state[GAIN_LOW, pair]
        out[pair] = fresh.astype(BF16)
        state[OUT_EVEN_LOW, pair] = fresh
        state[EVEN_INFLOW, pair] = jnp.zeros(fresh.shape, F32)


def tails_of(low, high, state, tails):
    pairs = state.shape[1]
    for layer, (links, row) in enumerate(((low, OUT_ODD_LOW), (high, OUT_ODD_HIGH))):
        tails[layer] = (state[row, pairs - 1] * link_of(links, 2 * pairs - 1)).astype(BF16)


def tails_kernel(stage_of_turn, recv, link, link_x, packed, packed_x, state_in, state, tails):
    stage, core = place()
    pair = recv.shape[0] - 1

    def work(low, high):
        state[OUT_ODD_HIGH, pair] = state[REST_HIGH, pair] - times_turned(
            recv[pair], high[1][CHAIN, 2 * pair + 1]
        )
        tails_of(low[0], high[0], state, tails)

    ordered(stage == stage_of_turn, core, (link, packed), (link_x, packed_x), work)


def first_tails_kernel(link, link_x, state_in, state, tails):
    _, core = place()
    ordered(True, core, link, link_x, lambda low, high: tails_of(low, high, state, tails))


def settle_gain(state, low, high, pair):
    high_gain = times(state[GAIN_HIGH, pair], high[INVERSE, 2 * pair])
    low_gain = times(state[GAIN_LOW, pair], low[INVERSE, 2 * pair])
    state[GAIN_HIGH, pair] = high_gain
    state[GAIN_LOW, pair] = low_gain - times_turned(high_gain, low[CHAIN, 2 * pair])


def even_gain_kernel(
    stage_of_turn, first, recv, link, link_x, forward, packed, packed_x, state_in, state
):
    stage, core = place()
    pairs = recv.shape[0]

    def work(low, high):
        if not first:
            for pair in range(pairs - 1):
                state[OUT_ODD_HIGH, pair] = state[REST_HIGH, pair] - times_turned(
                    recv[pair], high[0][CHAIN, 2 * pair + 1]
                )
        for layer, (blocks, links) in enumerate((low, high)):
            near, odd, gain = (
                (EVEN_LOW, OUT_ODD_LOW, GAIN_LOW),
                (EVEN_HIGH, OUT_ODD_HIGH, GAIN_HIGH),
            )[layer]
            for pair in range(pairs):
                fresh = forward[near, pair]
                if pair > 0:
                    fresh = fresh - link_of(links, 2 * pair - 1) * times(
                        state[odd, pair - 1], blocks[SIDE, 2 * pair]
                    )
                fresh = fresh - link_of(links, 2 * pair) * times(
                    state[odd, pair], blocks[SIDE, 2 * pair + 1]
                )
                state[gain, pair] = fresh
        for pair in range(1, pairs):
            settle_gain(state, low[0], high[0], pair)

    ordered(stage == stage_of_turn, core, (packed, link), (packed_x, link_x), work)


def even_first_kernel(stage_of_turn, tails, packed, packed_x, state_in, state):
    stage, core = place()

    def work(low, high):
        for layer, blocks in enumerate((low, high)):
            gain = (GAIN_LOW, GAIN_HIGH)[layer]
            state[gain, 0] = state[gain, 0] - times(tails[layer], blocks[SIDE, 0])
        settle_gain(state, low, high, 0)

    ordered(stage == stage_of_turn, core, packed, packed_x, work)


def split_kernel(state, packed, packed_x, kept, sent):
    _, core = place()
    pairs = state.shape[1]

    def work(low, high):
        for pair in range(pairs):
            even_high = state[GAIN_HIGH, pair] - times_turned(
                state[EVEN_INFLOW, pair], high[CHAIN, 2 * pair]
            )
            if low is packed:
                kept[2 * pair] = state[OUT_EVEN_LOW, pair]
                kept[2 * pair + 1] = state[OUT_ODD_LOW, pair]
                sent[2 * pair] = even_high.astype(BF16)
                sent[2 * pair + 1] = state[OUT_ODD_HIGH, pair].astype(BF16)
            else:
                sent[2 * pair] = state[OUT_EVEN_LOW, pair].astype(BF16)
                sent[2 * pair + 1] = state[OUT_ODD_LOW, pair].astype(BF16)
                kept[2 * pair] = even_high
                kept[2 * pair + 1] = state[OUT_ODD_HIGH, pair]

    ordered(True, core, packed, packed_x, work)


def join_kernel(kept, arrived, result):
    _, core = place()
    cells, half = kept.shape[0], kept.shape[1]
    for cell in range(cells):
        result[cell, half_rows(core, half), :] = kept[cell]
        result[cell, half_rows(1 - core, half), :] = arrived[cell].astype(F32)


def shards(rhs, dinv, lower_up, lower_span, upper_down, upper_span, span_link):
    rhs, dinv, lower_up = rhs[0], dinv[0], lower_up[0]
    lower_span, upper_down, upper_span = lower_span[0], upper_down[0], upper_span[0]
    cells, vecs, width = rhs.shape
    pairs, half = cells // 2, vecs // 2
    streams, spans = lax.axis_size("stream"), lax.axis_size("span")
    last = streams // 2 - 1

    def swapped(value):
        return lax.ppermute(value, "stream", [(index, index ^ 1) for index in range(streams)])

    def hop(value, start, end):
        return lax.ppermute(
            value, "stream", [(2 * start + core, 2 * end + core) for core in (0, 1)]
        )

    def beside(value, stage, step):
        links = []
        for member in range(stage % SPAN_PERIOD, last + 1, SPAN_PERIOD):
            for core in (0, 1):
                for span in range(spans):
                    if 0 <= span + step < spans:
                        base = (2 * member + core) * spans + span
                        links.append((base, base + step))
        return lax.ppermute(value, ("stream", "span"), links)

    def in_hbm(value):
        return pltpu.with_memory_space_constraint(value, pltpu.HBM)

    def after(value, *others):
        return lax.optimization_barrier((value,) + others)[0]

    part = functools.partial
    vectors = ((pairs, half, width), BF16)
    edges = ((2, half, width), BF16)
    forward_shape = ((6, pairs, half, width), F32)
    backward_shape = ((8, pairs, half, width), F32)
    blocks = ((cells, width, width), BF16)
    packed_shape = ((cells, half, width), F32)
    lower_shape = ((pairs, width, width), BF16)

    source, packed, lower_even, lower_odd = run(
        load_kernel, [packed_shape, packed_shape, lower_shape, lower_shape],
        in_hbm(rhs), in_hbm(lower_up.reshape(pairs, 2, width, width)), hbm=(0, 1),
        scratch=[pltpu.SemaphoreType.DMA] * 4,
    )
    source_x = swapped(packed)
    lower_even_x = swapped(lower_even)
    lower_odd_x = swapped(after(lower_odd, source_x))
    side_x = swapped(after(lower_span, lower_even_x, source_x))
    link_x = swapped(after(span_link, lower_odd_x))
    rows = (source, source_x)
    links = (span_link, link_x)
    evens = (lower_even, lower_even_x)
    odds = (lower_odd, lower_odd_x)
    sides = (lower_span, side_x)

    def even_turn(turn, recv, state):
        if turn == GATHER_TURN:
            state, out, packed = run(
                even_gather_kernel, [forward_shape, vectors, packed_shape], recv, both_even,
                *backs, state, early, alias={5: 0, 6: 2}, hbm=(2, 3, 4), **gathering,
            )
            packs.extend((packed, swapped(packed)))
        else:
            outs = [forward_shape, vectors][: 2 if turn < last else 1]
            state, *out = run(
                part(even_kernel, turn), outs, recv, both_even, state, alias={2: 0}
            )
            out = out[0] if turn < last else None
        sent = hop(out, turn, turn + 1) if turn < last else None
        state, heads = run(
            part(heads_kernel, turn), [forward_shape, edges], recv, *evens, state, alias={3: 0}
        )
        return state, sent, beside(heads, turn, -1)

    def odd_ready(turn, recv, heads, state):
        (state,) = run(
            part(odd_source_kernel, turn), [forward_shape], recv, *rows, *links, *evens, *odds,
            *sides, state, alias={11: 0},
        )
        (state,) = run(
            part(odd_last_kernel, turn), [forward_shape], heads, *links, *odds, *sides, state,
            alias={7: 0},
        )
        return state

    def odd_turn(turn, recv, state):
        outs = [forward_shape, vectors][: 2 if turn < last else 1]
        state, *out = run(part(odd_kernel, turn), outs, recv, both_odd, state, alias={2: 0})
        return state, hop(out[0], turn, turn + 1) if turn < last else None

    backs = (
        in_hbm(dinv), in_hbm(upper_down), in_hbm(upper_span.reshape(cells, width, width))
    )
    gathering = dict(
        scratch=[pltpu.VMEM((cells, width, width), BF16)] + [pltpu.SemaphoreType.DMA] * 3
    )
    packed_shape = ((3, cells, width, width), BF16)
    packs = []

    state, out = run(first_kernel, [forward_shape, vectors], *rows, *evens)
    even_recv = hop(out, 0, 1)
    state, heads = run(first_heads_kernel, [forward_shape, edges], state, alias={0: 0})
    heads = beside(heads, 0, -1)
    both_even, early = run(
        gather_early_kernel, [lower_shape, packed_shape], *evens, *backs, hbm=(2, 3, 4),
        **gathering,
    )
    state = odd_ready(0, out, heads, after(state, both_even))
    state, out = run(first_odd_kernel, [forward_shape, vectors], state, alias={0: 0})
    odd_recv = hop(out, 0, 1)
    here = even_recv
    state, even_recv, heads = even_turn(1, here, state)
    (both_odd,) = run(ahead_kernel, [lower_shape], after(lower_odd, state), lower_odd_x)
    state = odd_ready(1, here, heads, after(state, both_odd))
    state, odd_recv = odd_turn(1, odd_recv, state)
    for turn in range(2, last):
        here = even_recv
        state, even_recv, heads = even_turn(turn, here, state)
        state = odd_ready(turn, here, heads, state)
        if turn == last - 1:
            here = even_recv
            state, _, heads = even_turn(last, here, state)
        state, odd_recv = odd_turn(turn, odd_recv, state)
    state = odd_ready(last, here, heads, state)
    forward, _ = odd_turn(last, odd_recv, state)

    def back_odd_turn(stage, recv, state):
        outs = [backward_shape, vectors][: 2 if stage > 0 else 1]
        state, *out = run(part(odd_low_kernel, stage), outs, recv, both_odd, state, alias={2: 0})
        sent = hop(out[0], stage, stage - 1) if stage > 0 else None
        state, tails = run(
            part(tails_kernel, stage), [backward_shape, edges], recv, *links, *packs, state,
            alias={5: 0},
        )
        return state, sent, beside(tails, stage, 1)

    def even_ready(stage, recv, tails, state):
        (state,) = run(
            part(even_gain_kernel, stage, stage == last), [backward_shape], recv, *links, forward,
            *packs, state, alias={6: 0},
        )
        (state,) = run(
            part(even_first_kernel, stage), [backward_shape], tails, *packs, state, alias={3: 0}
        )
        return state

    def back_even_turn(stage, recv, state):
        outs = [backward_shape, vectors][: 2 if stage > 0 else 1]
        state, *out = run(
            part(even_out_kernel, stage), outs, recv, both_even, state, alias={2: 0}
        )
        return state, hop(out[0], stage, stage - 1) if stage > 0 else None

    state, out = run(turn_back_kernel, [backward_shape, vectors], forward, *odds, *packs)
    odd_recv = hop(out, last, last - 1)
    state, tails = run(first_tails_kernel, [backward_shape, edges], *links, state, alias={2: 0})
    tails = beside(tails, last, 1)
    both_even, both_odd = run(part(back_product_kernel, last), [lower_shape] * 2, *packs)
    state = even_ready(last, out, tails, after(state, both_odd))
    state, out = run(first_even_out_kernel, [backward_shape, vectors], state, alias={0: 0})
    even_recv = hop(out, last, last - 1)
    for stage in range(last - 1, -1, -1):
        here = odd_recv
        state, odd_recv, tails = back_odd_turn(stage, here, state)
        state = even_ready(stage, here, tails, state)
        state, even_recv = back_even_turn(stage, even_recv, state)

    kept, sent = run(
        split_kernel, [((cells, half, width), F32), ((cells, half, width), BF16)], state, *packs
    )
    arrived = swapped(sent)
    in_vmem = pl.BlockSpec(memory_space=pltpu.VMEM)
    result = pl.pallas_call(
        join_kernel,
        out_shape=jax.ShapeDtypeStruct((cells, vecs, width), F32),
        in_specs=[in_vmem] * 2,
        out_specs=in_vmem,
        compiler_params=pltpu.CompilerParams(vmem_limit_bytes=LIMIT),
    )(kept, arrived)
    return result[None]


def solution(mesh):
    return jax.shard_map(
        shards,
        mesh=mesh,
        in_specs=(
            P("stream", "span", None, None),
            P("stream", "span", None, None),
            P("stream", "span", None, None),
            P("stream", "span", None, None, None),
            P("stream", "span", None, None),
            P("stream", "span", None, None, None),
            P("stream", "span"),
        ),
        out_specs=P("stream", "span", None, None),
        check_vma=False,
    )
```

```python
import functools
import jax
import jax.numpy as jnp
from jax import lax
from jax.experimental import pallas as pl
from jax.experimental.pallas import tpu as pltpu
from jax.sharding import PartitionSpec as P

F32 = jnp.float32
BF16 = jnp.bfloat16
LIMIT = 10 * 1024 * 1024
SPAN_PERIOD = 4
GATHER_TURN = 4
GATHER_FROM = 3
CHAIN, INVERSE, SIDE = range(3)

EVEN_LOW, EVEN_HIGH, ODD_LOW, ODD_HIGH, ODD_PART, ODD_INFLOW = range(6)
REST_LOW, REST_HIGH, OUT_ODD_LOW, OUT_ODD_HIGH, GAIN_LOW, GAIN_HIGH, OUT_EVEN_LOW, EVEN_INFLOW = range(8)


def times(vectors, block):
    return lax.dot_general(
        vectors.astype(BF16), block, (((1,), (1,)), ((), ())), preferred_element_type=F32
    )


def product(left, right):
    return lax.dot_general(left, right, (((1,), (0,)), ((), ())), preferred_element_type=F32)


def turned_product(left, right):
    return lax.dot_general(right, left, (((0,), (1,)), ((), ())), preferred_element_type=F32)


def times_turned(vectors, block):
    return product(vectors.astype(BF16), block)


def run(body, outs, *operands, alias=None, hbm=(), scratch=()):
    in_vmem = pl.BlockSpec(memory_space=pltpu.VMEM)
    in_hbm = pl.BlockSpec(memory_space=pltpu.HBM)
    return pl.pallas_call(
        body,
        out_shape=[pltpu.VMEM(shape, dtype) for shape, dtype in outs],
        in_specs=[in_hbm if index in hbm else in_vmem for index in range(len(operands))],
        out_specs=[in_vmem] * len(outs),
        input_output_aliases=alias or {},
        scratch_shapes=list(scratch),
        compiler_params=pltpu.CompilerParams(vmem_limit_bytes=LIMIT),
    )(*operands)


def place():
    stream = lax.axis_index("stream")
    return stream // 2, stream % 2


def ordered(active, core, own, other, work):
    @pl.when(active & (core == 0))
    def _():
        work(own, other)

    @pl.when(active & (core == 1))
    def _():
        work(other, own)


def half_rows(core, half):
    return pl.ds(pl.multiple_of(core * half, half), half)


def load_kernel(rhs, lower, own, sent, even, odd, *sems):
    _, core = place()
    half = own.shape[1]
    copies = [
        (rhs.at[:, half_rows(1 - core, half), :], sent),
        (lower.at[:, 0], even),
        (lower.at[:, 1], odd),
        (rhs.at[:, half_rows(core, half), :], own),
    ]
    copies = [pltpu.make_async_copy(*ends, sem) for ends, sem in zip(copies, sems)]
    for copy in copies:
        copy.start()
    for copy in copies:
        copy.wait()


def first_kernel(source, source_x, lower, lower_x, state, out):
    _, core = place()
    pairs = out.shape[0]

    def work(low, high):
        for pair in range(pairs):
            fresh = high[0][2 * pair] - times(low[0][2 * pair], high[1][pair])
            out[pair] = fresh.astype(BF16)
            state[EVEN_HIGH, pair] = fresh
        for pair in range(pairs):
            state[EVEN_LOW, pair] = low[0][2 * pair]

    ordered(True, core, (source, lower), (source_x, lower_x), work)


def ahead_kernel(lower, lower_x, both):
    stage, core = place()

    def work(low, high):
        for pair in range(both.shape[0]):
            both[pair] = turned_product(high[pair], low[pair]).astype(BF16)

    ordered(stage > 0, core, lower, lower_x, work)


def gather_back(inverse, upper, side, packed, upper_here, sems):
    copies = [
        pltpu.make_async_copy(upper, upper_here, sems[0]),
        pltpu.make_async_copy(inverse, packed.at[INVERSE], sems[1]),
        pltpu.make_async_copy(side, packed.at[SIDE], sems[2]),
    ]
    for copy in copies:
        copy.start()
    for copy in copies:
        copy.wait()
    for cell in range(packed.shape[1]):
        packed[CHAIN, cell] = turned_product(packed[INVERSE, cell], upper_here[cell]).astype(BF16)


def gather_early_kernel(
    even, even_x, inverse, upper, side, both, packed, upper_here, *sems
):
    stage, _ = place()
    ahead_kernel(even, even_x, both)

    @pl.when(stage >= GATHER_FROM)
    def _():
        gather_back(inverse, upper, side, packed, upper_here, sems)


def even_kernel(turn, recv, both, state_in, state, out=None):
    stage, _ = place()

    @pl.when(stage == turn)
    def _():
        for pair in range(recv.shape[0]):
            fresh = state[EVEN_HIGH, pair] + times_turned(recv[pair], both[pair])
            if out is not None:
                out[pair] = fresh.astype(BF16)
            state[EVEN_HIGH, pair] = fresh


def back_product_kernel(last, packed, packed_x, both_even, both_odd):
    stage, core = place()

    def work(low, high):
        for parity, both in enumerate((both_even, both_odd)):
            for pair in range(both.shape[0]):
                cell = 2 * pair + parity
                both[pair] = product(high[CHAIN, cell], low[CHAIN, cell]).astype(BF16)

    ordered(stage < last, core, packed, packed_x, work)


def even_gather_kernel(
    recv, both, inverse, upper, side, state_in, packed_in, state, out, packed, upper_here, *sems
):
    stage, _ = place()
    even_kernel(GATHER_TURN, recv, both, state_in, state, out)

    @pl.when(stage < GATHER_FROM)
    def _():
        gather_back(inverse, upper, side, packed, upper_here, sems)


def heads_kernel(turn, recv, lower, lower_x, state_in, state, heads):
    stage, core = place()

    def work(low, high):
        state[EVEN_LOW, 0] = state[EVEN_LOW, 0] - times(recv[0], low[0])
        heads[0] = state[EVEN_LOW, 0].astype(BF16)
        heads[1] = state[EVEN_HIGH, 0].astype(BF16)

    ordered(stage == turn, core, lower, lower_x, work)


def first_heads_kernel(state_in, state, heads):
    heads[0] = state[EVEN_LOW, 0].astype(BF16)
    heads[1] = state[EVEN_HIGH, 0].astype(BF16)


def link_of(link, cell):
    return link[0:1, cell : cell + 1].astype(F32)


def odd_source_kernel(
    turn, recv, source, source_x, link, link_x, even, even_x, odd, odd_x, side, side_x,
    state_in, state
):
    stage, core = place()
    pairs = side.shape[0]

    def work(low, high):
        if turn > 0:
            for pair in range(1, pairs):
                state[EVEN_LOW, pair] = state[EVEN_LOW, pair] - times(recv[pair], low[1][pair])
        for layer, (values, _, _, sides, links) in enumerate((low, high)):
            near, row = ((EVEN_LOW, ODD_LOW), (EVEN_HIGH, ODD_PART))[layer]
            for pair in range(pairs):
                fresh = values[2 * pair + 1]
                fresh = fresh - link_of(links, 2 * pair) * times(
                    state[near, pair], sides[pair, 0]
                )
                if pair + 1 < pairs:
                    fresh = fresh - link_of(links, 2 * pair + 1) * times(
                        state[near, pair + 1], sides[pair, 1]
                    )
                state[row, pair] = fresh
        for pair in range(pairs - 1):
            state[ODD_PART, pair] = state[ODD_PART, pair] - times(
                state[ODD_LOW, pair], high[2][pair]
            )

    ordered(
        stage == turn, core,
        (source, even, odd, side, link), (source_x, even_x, odd_x, side_x, link_x), work,
    )


def odd_last_kernel(turn, heads, link, link_x, odd, odd_x, side, side_x, state_in, state):
    stage, core = place()
    pair = side.shape[0] - 1

    def work(low, high):
        for layer, (links, _, sides) in enumerate((low, high)):
            row = (ODD_LOW, ODD_PART)[layer]
            state[row, pair] = state[row, pair] - link_of(links, 2 * pair + 1) * times(
                heads[layer], sides[pair, 1]
            )
        state[ODD_PART, pair] = state[ODD_PART, pair] - times(
            state[ODD_LOW, pair], high[1][pair]
        )

    ordered(stage == turn, core, (link, odd, side), (link_x, odd_x, side_x), work)


def odd_kernel(turn, recv, both, state_in, state, out=None):
    stage, _ = place()

    @pl.when(stage == turn)
    def _():
        for pair in range(recv.shape[0]):
            fresh = state[ODD_PART, pair] + times_turned(recv[pair], both[pair])
            if out is not None:
                out[pair] = fresh.astype(BF16)
            state[ODD_HIGH, pair] = fresh
            state[ODD_INFLOW, pair] = recv[pair].astype(F32)


def first_odd_kernel(state_in, state, out):
    for pair in range(out.shape[0]):
        fresh = state[ODD_PART, pair]
        out[pair] = fresh.astype(BF16)
        state[ODD_HIGH, pair] = fresh
        state[ODD_INFLOW, pair] = jnp.zeros(fresh.shape, F32)


def odd_finish_kernel(
    turn, heads, recv, both, link, link_x, odd, odd_x, side, side_x, state_in, state, out
):
    odd_last_kernel(turn, heads, link, link_x, odd, odd_x, side, side_x, state_in, state)
    odd_kernel(turn, recv, both, state_in, state, out)


def odd_finish_first_kernel(
    heads, link, link_x, odd, odd_x, side, side_x, state_in, state, out
):
    odd_last_kernel(0, heads, link, link_x, odd, odd_x, side, side_x, state_in, state)
    stage, _ = place()

    @pl.when(stage == 0)
    def _():
        first_odd_kernel(state_in, state, out)


def odd_source_ahead_kernel(
    turn, recv, source, source_x, link, link_x, even, even_x, odd, odd_x, side, side_x,
    state_in, state, both
):
    ahead_kernel(odd, odd_x, both)
    odd_source_kernel(
        turn, recv, source, source_x, link, link_x, even, even_x, odd, odd_x, side, side_x,
        state_in, state,
    )


def turn_back_kernel(forward, lower, lower_x, packed, packed_x, state, out):
    _, core = place()
    pairs = out.shape[0]

    def work(low, high):
        for pair in range(pairs):
            cell = 2 * pair + 1
            high_rest = times(forward[ODD_HIGH, pair], high[1][INVERSE, cell])
            low_value = forward[ODD_LOW, pair] - times(forward[ODD_INFLOW, pair], low[0][pair])
            low_rest = times(low_value, low[1][INVERSE, cell])
            low_rest = low_rest - times_turned(high_rest, low[1][CHAIN, cell])
            state[REST_HIGH, pair] = high_rest
            state[OUT_ODD_HIGH, pair] = high_rest
            state[REST_LOW, pair] = low_rest
            state[OUT_ODD_LOW, pair] = low_rest
            out[pair] = low_rest.astype(BF16)

    ordered(True, core, (lower, packed), (lower_x, packed_x), work)


def odd_low_kernel(stage_of_turn, recv, both, state_in, state, out=None):
    stage, _ = place()

    @pl.when(stage == stage_of_turn)
    def _():
        for pair in range(recv.shape[0]):
            fresh = state[REST_LOW, pair] + times_turned(recv[pair], both[pair])
            if out is not None:
                out[pair] = fresh.astype(BF16)
            state[OUT_ODD_LOW, pair] = fresh


def even_out_kernel(stage_of_turn, recv, both, state_in, state, out=None):
    stage, _ = place()

    @pl.when(stage == stage_of_turn)
    def _():
        for pair in range(recv.shape[0]):
            fresh = state[GAIN_LOW, pair] + times_turned(recv[pair], both[pair])
            if out is not None:
                out[pair] = fresh.astype(BF16)
            state[OUT_EVEN_LOW, pair] = fresh
            state[EVEN_INFLOW, pair] = recv[pair].astype(F32)


def first_even_out_kernel(state_in, state, out):
    for pair in range(out.shape[0]):
        fresh = state[GAIN_LOW, pair]
        out[pair] = fresh.astype(BF16)
        state[OUT_EVEN_LOW, pair] = fresh
        state[EVEN_INFLOW, pair] = jnp.zeros(fresh.shape, F32)


def tails_of(low, high, state, tails):
    pairs = state.shape[1]
    for layer, (links, row) in enumerate(((low, OUT_ODD_LOW), (high, OUT_ODD_HIGH))):
        tails[layer] = (state[row, pairs - 1] * link_of(links, 2 * pairs - 1)).astype(BF16)


def tails_kernel(stage_of_turn, recv, link, link_x, packed, packed_x, state_in, state, tails):
    stage, core = place()
    pair = recv.shape[0] - 1

    def work(low, high):
        state[OUT_ODD_HIGH, pair] = state[REST_HIGH, pair] - times_turned(
            recv[pair], high[1][CHAIN, 2 * pair + 1]
        )
        tails_of(low[0], high[0], state, tails)

    ordered(stage == stage_of_turn, core, (link, packed), (link_x, packed_x), work)


def first_tails_kernel(link, link_x, state_in, state, tails):
    _, core = place()
    ordered(True, core, link, link_x, lambda low, high: tails_of(low, high, state, tails))


def settle_gain(state, low, high, pair):
    high_gain = times(state[GAIN_HIGH, pair], high[INVERSE, 2 * pair])
    low_gain = times(state[GAIN_LOW, pair], low[INVERSE, 2 * pair])
    state[GAIN_HIGH, pair] = high_gain
    state[GAIN_LOW, pair] = low_gain - times_turned(high_gain, low[CHAIN, 2 * pair])


def even_gain_kernel(
    stage_of_turn, first, recv, link, link_x, forward, packed, packed_x, state_in, state
):
    stage, core = place()
    pairs = recv.shape[0]

    def work(low, high):
        if not first:
            for pair in range(pairs - 1):
                state[OUT_ODD_HIGH, pair] = state[REST_HIGH, pair] - times_turned(
                    recv[pair], high[0][CHAIN, 2 * pair + 1]
                )
        for layer, (blocks, links) in enumerate((low, high)):
            near, odd, gain = (
                (EVEN_LOW, OUT_ODD_LOW, GAIN_LOW),
                (EVEN_HIGH, OUT_ODD_HIGH, GAIN_HIGH),
            )[layer]
            for pair in range(pairs):
                fresh = forward[near, pair]
                if pair > 0:
                    fresh = fresh - link_of(links, 2 * pair - 1) * times(
                        state[odd, pair - 1], blocks[SIDE, 2 * pair]
                    )
                fresh = fresh - link_of(links, 2 * pair) * times(
                    state[odd, pair], blocks[SIDE, 2 * pair + 1]
                )
                state[gain, pair] = fresh
        for pair in range(1, pairs):
            settle_gain(state, low[0], high[0], pair)

    ordered(stage == stage_of_turn, core, (packed, link), (packed_x, link_x), work)


def even_first_kernel(stage_of_turn, tails, packed, packed_x, state_in, state):
    stage, core = place()

    def work(low, high):
        for layer, blocks in enumerate((low, high)):
            gain = (GAIN_LOW, GAIN_HIGH)[layer]
            state[gain, 0] = state[gain, 0] - times(tails[layer], blocks[SIDE, 0])
        settle_gain(state, low, high, 0)

    ordered(stage == stage_of_turn, core, packed, packed_x, work)


def split_kernel(state, packed, packed_x, kept, sent):
    _, core = place()
    pairs = state.shape[1]

    def work(low, high):
        for pair in range(pairs):
            even_high = state[GAIN_HIGH, pair] - times_turned(
                state[EVEN_INFLOW, pair], high[CHAIN, 2 * pair]
            )
            if low is packed:
                kept[2 * pair] = state[OUT_EVEN_LOW, pair]
                kept[2 * pair + 1] = state[OUT_ODD_LOW, pair]
                sent[2 * pair] = even_high.astype(BF16)
                sent[2 * pair + 1] = state[OUT_ODD_HIGH, pair].astype(BF16)
            else:
                sent[2 * pair] = state[OUT_EVEN_LOW, pair].astype(BF16)
                sent[2 * pair + 1] = state[OUT_ODD_LOW, pair].astype(BF16)
                kept[2 * pair] = even_high
                kept[2 * pair + 1] = state[OUT_ODD_HIGH, pair]

    ordered(True, core, packed, packed_x, work)


def join_kernel(kept, arrived, result):
    _, core = place()
    cells, half = kept.shape[0], kept.shape[1]
    for cell in range(cells):
        result[cell, half_rows(core, half), :] = kept[cell]
        result[cell, half_rows(1 - core, half), :] = arrived[cell].astype(F32)


def shards(rhs, dinv, lower_up, lower_span, upper_down, upper_span, span_link):
    rhs, dinv, lower_up = rhs[0], dinv[0], lower_up[0]
    lower_span, upper_down, upper_span = lower_span[0], upper_down[0], upper_span[0]
    cells, vecs, width = rhs.shape
    pairs, half = cells // 2, vecs // 2
    streams, spans = lax.axis_size("stream"), lax.axis_size("span")
    last = streams // 2 - 1

    def swapped(value):
        return lax.ppermute(value, "stream", [(index, index ^ 1) for index in range(streams)])

    def hop(value, start, end):
        return lax.ppermute(
            value, "stream", [(2 * start + core, 2 * end + core) for core in (0, 1)]
        )

    def beside(value, stage, step):
        links = []
        for member in range(stage % SPAN_PERIOD, last + 1, SPAN_PERIOD):
            for core in (0, 1):
                for span in range(spans):
                    if 0 <= span + step < spans:
                        base = (2 * member + core) * spans + span
                        links.append((base, base + step))
        return lax.ppermute(value, ("stream", "span"), links)

    def in_hbm(value):
        return pltpu.with_memory_space_constraint(value, pltpu.HBM)

    def after(value, *others):
        return lax.optimization_barrier((value,) + others)[0]

    part = functools.partial
    vectors = ((pairs, half, width), BF16)
    edges = ((2, half, width), BF16)
    forward_shape = ((6, pairs, half, width), F32)
    backward_shape = ((8, pairs, half, width), F32)
    blocks = ((cells, width, width), BF16)
    packed_shape = ((cells, half, width), F32)
    lower_shape = ((pairs, width, width), BF16)

    source, packed, lower_even, lower_odd = run(
        load_kernel, [packed_shape, packed_shape, lower_shape, lower_shape],
        in_hbm(rhs), in_hbm(lower_up.reshape(pairs, 2, width, width)), hbm=(0, 1),
        scratch=[pltpu.SemaphoreType.DMA] * 4,
    )
    source_x = swapped(packed)
    lower_even_x = swapped(lower_even)
    lower_odd_x = swapped(after(lower_odd, source_x))
    side_x = swapped(after(lower_span, lower_even_x, source_x))
    link_x = swapped(after(span_link, lower_even_x))
    rows = (source, source_x)
    links = (span_link, link_x)
    evens = (lower_even, lower_even_x)
    odds = (lower_odd, lower_odd_x)
    sides = (lower_span, side_x)

    def even_turn(turn, recv, state):
        if turn == GATHER_TURN:
            state, out, packed = run(
                even_gather_kernel, [forward_shape, vectors, packed_shape], recv, both_even,
                *backs, state, early, alias={5: 0, 6: 2}, hbm=(2, 3, 4), **gathering,
            )
            packs.extend((packed, swapped(packed)))
        else:
            outs = [forward_shape, vectors][: 2 if turn < last else 1]
            state, *out = run(
                part(even_kernel, turn), outs, recv, both_even, state, alias={2: 0}
            )
            out = out[0] if turn < last else None
        sent = hop(out, turn, turn + 1) if turn < last else None
        state, heads = run(
            part(heads_kernel, turn), [forward_shape, edges], recv, *evens, state, alias={3: 0}
        )
        return state, sent, beside(heads, turn, -1)

    def odd_ready(turn, recv, heads, state):
        (state,) = run(
            part(odd_source_kernel, turn), [forward_shape], recv, *rows, *links, *evens, *odds,
            *sides, state, alias={11: 0},
        )
        (state,) = run(
            part(odd_last_kernel, turn), [forward_shape], heads, *links, *odds, *sides, state,
            alias={7: 0},
        )
        return state

    def odd_turn(turn, recv, state):
        outs = [forward_shape, vectors][: 2 if turn < last else 1]
        state, *out = run(part(odd_kernel, turn), outs, recv, both_odd, state, alias={2: 0})
        return state, hop(out[0], turn, turn + 1) if turn < last else None

    backs = (
        in_hbm(dinv), in_hbm(upper_down), in_hbm(upper_span.reshape(cells, width, width))
    )
    gathering = dict(
        scratch=[pltpu.VMEM((cells, width, width), BF16)] + [pltpu.SemaphoreType.DMA] * 3
    )
    packed_shape = ((3, cells, width, width), BF16)
    packs = []

    state, out = run(first_kernel, [forward_shape, vectors], *rows, *evens)
    even_recv = hop(out, 0, 1)
    state, heads = run(first_heads_kernel, [forward_shape, edges], state, alias={0: 0})
    heads = beside(heads, 0, -1)
    both_even, early = run(
        gather_early_kernel, [lower_shape, packed_shape], *evens, *backs, hbm=(2, 3, 4),
        **gathering,
    )
    here = even_recv
    state, even_recv, next_heads = even_turn(1, here, after(state, both_even))
    (state,) = run(
        part(odd_source_kernel, 0), [forward_shape], out, *rows, *links, *evens, *odds, *sides,
        state, alias={11: 0},
    )
    state, out = run(
        odd_finish_first_kernel, [forward_shape, vectors], heads, *links, *odds, *sides, state,
        alias={7: 0},
    )
    odd_recv = hop(out, 0, 1)
    state, both_odd = run(
        part(odd_source_ahead_kernel, 1), [forward_shape, lower_shape], here, *rows, *links,
        *evens, *odds, *sides, state, alias={11: 0},
    )
    state, out = run(
        part(odd_finish_kernel, 1), [forward_shape, vectors], next_heads, odd_recv, both_odd,
        *links, *odds, *sides, state, alias={9: 0},
    )
    odd_recv = hop(out, 1, 2)
    for turn in range(2, last):
        here = even_recv
        state, even_recv, heads = even_turn(turn, here, state)
        state = odd_ready(turn, here, heads, state)
        if turn == last - 1:
            here = even_recv
            state, _, heads = even_turn(last, here, state)
        state, odd_recv = odd_turn(turn, odd_recv, state)
    state = odd_ready(last, here, heads, state)
    forward, _ = odd_turn(last, odd_recv, state)

    def back_odd_turn(stage, recv, state):
        outs = [backward_shape, vectors][: 2 if stage > 0 else 1]
        state, *out = run(part(odd_low_kernel, stage), outs, recv, both_odd, state, alias={2: 0})
        sent = hop(out[0], stage, stage - 1) if stage > 0 else None
        state, tails = run(
            part(tails_kernel, stage), [backward_shape, edges], recv, *links, *packs, state,
            alias={5: 0},
        )
        return state, sent, beside(tails, stage, 1)

    def even_ready(stage, recv, tails, state):
        (state,) = run(
            part(even_gain_kernel, stage, stage == last), [backward_shape], recv, *links, forward,
            *packs, state, alias={6: 0},
        )
        (state,) = run(
            part(even_first_kernel, stage), [backward_shape], tails, *packs, state, alias={3: 0}
        )
        return state

    def back_even_turn(stage, recv, state):
        outs = [backward_shape, vectors][: 2 if stage > 0 else 1]
        state, *out = run(
            part(even_out_kernel, stage), outs, recv, both_even, state, alias={2: 0}
        )
        return state, hop(out[0], stage, stage - 1) if stage > 0 else None

    state, out = run(turn_back_kernel, [backward_shape, vectors], forward, *odds, *packs)
    odd_recv = hop(out, last, last - 1)
    state, tails = run(first_tails_kernel, [backward_shape, edges], *links, state, alias={2: 0})
    tails = beside(tails, last, 1)
    both_even, both_odd = run(part(back_product_kernel, last), [lower_shape] * 2, *packs)
    state = even_ready(last, out, tails, after(state, both_odd))
    state, out = run(first_even_out_kernel, [backward_shape, vectors], state, alias={0: 0})
    even_recv = hop(out, last, last - 1)
    for stage in range(last - 1, -1, -1):
        here = odd_recv
        state, odd_recv, tails = back_odd_turn(stage, here, state)
        state = even_ready(stage, here, tails, state)
        state, even_recv = back_even_turn(stage, even_recv, state)

    kept, sent = run(
        split_kernel, [((cells, half, width), F32), ((cells, half, width), BF16)], state, *packs
    )
    arrived = swapped(sent)
    in_vmem = pl.BlockSpec(memory_space=pltpu.VMEM)
    result = pl.pallas_call(
        join_kernel,
        out_shape=jax.ShapeDtypeStruct((cells, vecs, width), F32),
        in_specs=[in_vmem] * 2,
        out_specs=in_vmem,
        compiler_params=pltpu.CompilerParams(vmem_limit_bytes=LIMIT),
    )(kept, arrived)
    return result[None]


def solution(mesh):
    return jax.shard_map(
        shards,
        mesh=mesh,
        in_specs=(
            P("stream", "span", None, None),
            P("stream", "span", None, None),
            P("stream", "span", None, None),
            P("stream", "span", None, None, None),
            P("stream", "span", None, None),
            P("stream", "span", None, None, None),
            P("stream", "span"),
        ),
        out_specs=P("stream", "span", None, None),
        check_vma=False,
    )
```

```python
import functools
import jax
import jax.numpy as jnp
from jax import lax
from jax.experimental import pallas as pl
from jax.experimental.pallas import tpu as pltpu
from jax.sharding import PartitionSpec as P

F32 = jnp.float32
BF16 = jnp.bfloat16
LIMIT = 10 * 1024 * 1024
SPAN_PERIOD = 4
GATHER_TURN = 6
GATHER_FROM = 5
CHAIN, INVERSE, SIDE = range(3)

EVEN_LOW, EVEN_HIGH, ODD_LOW, ODD_HIGH, ODD_PART, ODD_INFLOW = range(6)
REST_LOW, REST_HIGH, OUT_ODD_LOW, OUT_ODD_HIGH, GAIN_LOW, GAIN_HIGH, OUT_EVEN_LOW, EVEN_INFLOW = range(8)


def times(vectors, block):
    return lax.dot_general(
        vectors.astype(BF16), block, (((1,), (1,)), ((), ())), preferred_element_type=F32
    )


def product(left, right):
    return lax.dot_general(left, right, (((1,), (0,)), ((), ())), preferred_element_type=F32)


def turned_product(left, right):
    return lax.dot_general(right, left, (((0,), (1,)), ((), ())), preferred_element_type=F32)


def times_turned(vectors, block):
    return product(vectors.astype(BF16), block)


def run(body, outs, *operands, alias=None, hbm=(), scratch=()):
    in_vmem = pl.BlockSpec(memory_space=pltpu.VMEM)
    in_hbm = pl.BlockSpec(memory_space=pltpu.HBM)
    return pl.pallas_call(
        body,
        out_shape=[pltpu.VMEM(shape, dtype) for shape, dtype in outs],
        in_specs=[in_hbm if index in hbm else in_vmem for index in range(len(operands))],
        out_specs=[in_vmem] * len(outs),
        input_output_aliases=alias or {},
        scratch_shapes=list(scratch),
        compiler_params=pltpu.CompilerParams(vmem_limit_bytes=LIMIT),
    )(*operands)


def place():
    stream = lax.axis_index("stream")
    return stream // 2, stream % 2


def ordered(active, core, own, other, work):
    @pl.when(active & (core == 0))
    def _():
        work(own, other)

    @pl.when(active & (core == 1))
    def _():
        work(other, own)


def half_rows(core, half):
    return pl.ds(pl.multiple_of(core * half, half), half)


def load_kernel(rhs, lower, own, sent, even, odd, *sems):
    _, core = place()
    half = own.shape[1]
    copies = [
        (rhs.at[:, half_rows(1 - core, half), :], sent),
        (lower.at[:, 0], even),
        (lower.at[:, 1], odd),
        (rhs.at[:, half_rows(core, half), :], own),
    ]
    copies = [pltpu.make_async_copy(*ends, sem) for ends, sem in zip(copies, sems)]
    for copy in copies:
        copy.start()
    for copy in copies:
        copy.wait()


def first_kernel(source, source_x, lower, lower_x, state, out):
    _, core = place()
    pairs = out.shape[0]

    def work(low, high):
        for pair in range(pairs):
            fresh = high[0][2 * pair] - times(low[0][2 * pair], high[1][pair])
            out[pair] = fresh.astype(BF16)
            state[EVEN_HIGH, pair] = fresh
        for pair in range(pairs):
            state[EVEN_LOW, pair] = low[0][2 * pair]

    ordered(True, core, (source, lower), (source_x, lower_x), work)


def ahead_kernel(lower, lower_x, both):
    stage, core = place()

    def work(low, high):
        for pair in range(both.shape[0]):
            both[pair] = turned_product(high[pair], low[pair]).astype(BF16)

    ordered(stage > 0, core, lower, lower_x, work)


def gather_back(inverse, upper, side, packed, upper_here, sems):
    copies = [
        pltpu.make_async_copy(upper, upper_here, sems[0]),
        pltpu.make_async_copy(inverse, packed.at[INVERSE], sems[1]),
        pltpu.make_async_copy(side, packed.at[SIDE], sems[2]),
    ]
    for copy in copies:
        copy.start()
    for copy in copies:
        copy.wait()
    width = packed.shape[2]
    rows = lax.broadcasted_iota(jnp.int32, (width, width), 0)
    columns = lax.broadcasted_iota(jnp.int32, (width, width), 1)
    unit = jnp.where(rows == columns, 1.0, 0.0).astype(BF16)
    for cell in range(packed.shape[1]):
        packed[CHAIN, cell] = turned_product(packed[INVERSE, cell], upper_here[cell]).astype(BF16)
        packed[INVERSE, cell] = turned_product(unit, packed[INVERSE, cell]).astype(BF16)
        packed[SIDE, cell] = turned_product(unit, packed[SIDE, cell]).astype(BF16)


def gather_early_kernel(
    even, even_x, inverse, upper, side, both, packed, upper_here, *sems
):
    stage, _ = place()
    ahead_kernel(even, even_x, both)

    @pl.when(stage >= GATHER_FROM)
    def _():
        gather_back(inverse, upper, side, packed, upper_here, sems)


def even_kernel(turn, recv, both, state_in, state, out=None):
    stage, _ = place()

    @pl.when(stage == turn)
    def _():
        for pair in range(recv.shape[0]):
            fresh = state[EVEN_HIGH, pair] + times_turned(recv[pair], both[pair])
            if out is not None:
                out[pair] = fresh.astype(BF16)
            state[EVEN_HIGH, pair] = fresh


def back_product_kernel(last, packed, packed_x, both_even, both_odd):
    stage, core = place()

    def work(low, high):
        for parity, both in enumerate((both_even, both_odd)):
            for pair in range(both.shape[0]):
                cell = 2 * pair + parity
                both[pair] = product(high[CHAIN, cell], low[CHAIN, cell]).astype(BF16)

    ordered(stage < last, core, packed, packed_x, work)


def even_gather_kernel(
    recv, both, inverse, upper, side, state_in, packed_in, state, out, packed, upper_here, *sems
):
    stage, _ = place()
    even_kernel(GATHER_TURN, recv, both, state_in, state, out)

    @pl.when(stage < GATHER_FROM)
    def _():
        gather_back(inverse, upper, side, packed, upper_here, sems)


def heads_kernel(turn, recv, lower, lower_x, state_in, state, heads):
    stage, core = place()

    def work(low, high):
        state[EVEN_LOW, 0] = state[EVEN_LOW, 0] - times(recv[0], low[0])
        heads[0] = state[EVEN_LOW, 0].astype(BF16)
        heads[1] = state[EVEN_HIGH, 0].astype(BF16)

    ordered(stage == turn, core, lower, lower_x, work)


def first_heads_kernel(state_in, state, heads):
    heads[0] = state[EVEN_LOW, 0].astype(BF16)
    heads[1] = state[EVEN_HIGH, 0].astype(BF16)


def link_of(link, cell):
    return link[0:1, cell : cell + 1].astype(F32)


def odd_source_kernel(
    turn, recv, source, source_x, link, link_x, even, even_x, odd, odd_x, side, side_x,
    state_in, state
):
    stage, core = place()
    pairs = side.shape[0]

    def work(low, high):
        if turn > 0:
            for pair in range(1, pairs):
                state[EVEN_LOW, pair] = state[EVEN_LOW, pair] - times(recv[pair], low[1][pair])
        for layer, (values, _, _, sides, links) in enumerate((low, high)):
            near, row = ((EVEN_LOW, ODD_LOW), (EVEN_HIGH, ODD_PART))[layer]
            for pair in range(pairs):
                fresh = values[2 * pair + 1]
                fresh = fresh - link_of(links, 2 * pair) * times(
                    state[near, pair], sides[pair, 0]
                )
                if pair + 1 < pairs:
                    fresh = fresh - link_of(links, 2 * pair + 1) * times(
                        state[near, pair + 1], sides[pair, 1]
                    )
                state[row, pair] = fresh
        for pair in range(pairs - 1):
            state[ODD_PART, pair] = state[ODD_PART, pair] - times(
                state[ODD_LOW, pair], high[2][pair]
            )

    ordered(
        stage == turn, core,
        (source, even, odd, side, link), (source_x, even_x, odd_x, side_x, link_x), work,
    )


def odd_last_kernel(turn, heads, link, link_x, odd, odd_x, side, side_x, state_in, state):
    stage, core = place()
    pair = side.shape[0] - 1

    def work(low, high):
        for layer, (links, _, sides) in enumerate((low, high)):
            row = (ODD_LOW, ODD_PART)[layer]
            state[row, pair] = state[row, pair] - link_of(links, 2 * pair + 1) * times(
                heads[layer], sides[pair, 1]
            )
        state[ODD_PART, pair] = state[ODD_PART, pair] - times(
            state[ODD_LOW, pair], high[1][pair]
        )

    ordered(stage == turn, core, (link, odd, side), (link_x, odd_x, side_x), work)


def odd_kernel(turn, recv, both, state_in, state, out=None):
    stage, _ = place()

    @pl.when(stage == turn)
    def _():
        for pair in range(recv.shape[0]):
            fresh = state[ODD_PART, pair] + times_turned(recv[pair], both[pair])
            if out is not None:
                out[pair] = fresh.astype(BF16)
            state[ODD_HIGH, pair] = fresh
            state[ODD_INFLOW, pair] = recv[pair].astype(F32)


def first_odd_kernel(state_in, state, out):
    for pair in range(out.shape[0]):
        fresh = state[ODD_PART, pair]
        out[pair] = fresh.astype(BF16)
        state[ODD_HIGH, pair] = fresh
        state[ODD_INFLOW, pair] = jnp.zeros(fresh.shape, F32)


def odd_finish_kernel(
    turn, heads, recv, both, link, link_x, odd, odd_x, side, side_x, state_in, state, out
):
    odd_last_kernel(turn, heads, link, link_x, odd, odd_x, side, side_x, state_in, state)
    odd_kernel(turn, recv, both, state_in, state, out)


def odd_finish_first_kernel(
    heads, link, link_x, odd, odd_x, side, side_x, state_in, state, out
):
    odd_last_kernel(0, heads, link, link_x, odd, odd_x, side, side_x, state_in, state)
    stage, _ = place()

    @pl.when(stage == 0)
    def _():
        first_odd_kernel(state_in, state, out)


def odd_source_ahead_kernel(
    turn, recv, source, source_x, link, link_x, even, even_x, odd, odd_x, side, side_x,
    state_in, state, both
):
    ahead_kernel(odd, odd_x, both)
    odd_source_kernel(
        turn, recv, source, source_x, link, link_x, even, even_x, odd, odd_x, side, side_x,
        state_in, state,
    )


def turn_back_kernel(forward, lower, lower_x, packed, packed_x, state, out):
    _, core = place()
    pairs = out.shape[0]

    def work(low, high):
        for pair in range(pairs):
            cell = 2 * pair + 1
            high_rest = times_turned(forward[ODD_HIGH, pair], high[1][INVERSE, cell])
            low_value = forward[ODD_LOW, pair] - times(forward[ODD_INFLOW, pair], low[0][pair])
            low_rest = times_turned(low_value, low[1][INVERSE, cell])
            low_rest = low_rest - times_turned(high_rest, low[1][CHAIN, cell])
            state[REST_HIGH, pair] = high_rest
            state[OUT_ODD_HIGH, pair] = high_rest
            state[REST_LOW, pair] = low_rest
            state[OUT_ODD_LOW, pair] = low_rest
            out[pair] = low_rest.astype(BF16)

    ordered(True, core, (lower, packed), (lower_x, packed_x), work)


def odd_low_kernel(stage_of_turn, recv, both, state_in, state, out=None):
    stage, _ = place()

    @pl.when(stage == stage_of_turn)
    def _():
        for pair in range(recv.shape[0]):
            fresh = state[REST_LOW, pair] + times_turned(recv[pair], both[pair])
            if out is not None:
                out[pair] = fresh.astype(BF16)
            state[OUT_ODD_LOW, pair] = fresh


def even_out_kernel(stage_of_turn, recv, both, state_in, state, out=None):
    stage, _ = place()

    @pl.when(stage == stage_of_turn)
    def _():
        for pair in range(recv.shape[0]):
            fresh = state[GAIN_LOW, pair] + times_turned(recv[pair], both[pair])
            if out is not None:
                out[pair] = fresh.astype(BF16)
            state[OUT_EVEN_LOW, pair] = fresh
            state[EVEN_INFLOW, pair] = recv[pair].astype(F32)


def first_even_out_kernel(state_in, state, out):
    for pair in range(out.shape[0]):
        fresh = state[GAIN_LOW, pair]
        out[pair] = fresh.astype(BF16)
        state[OUT_EVEN_LOW, pair] = fresh
        state[EVEN_INFLOW, pair] = jnp.zeros(fresh.shape, F32)


def tails_of(low, high, state, tails):
    pairs = state.shape[1]
    for layer, (links, row) in enumerate(((low, OUT_ODD_LOW), (high, OUT_ODD_HIGH))):
        tails[layer] = (state[row, pairs - 1] * link_of(links, 2 * pairs - 1)).astype(BF16)


def tails_kernel(stage_of_turn, recv, link, link_x, packed, packed_x, state_in, state, tails):
    stage, core = place()
    pair = recv.shape[0] - 1

    def work(low, high):
        state[OUT_ODD_HIGH, pair] = state[REST_HIGH, pair] - times_turned(
            recv[pair], high[1][CHAIN, 2 * pair + 1]
        )
        tails_of(low[0], high[0], state, tails)

    ordered(stage == stage_of_turn, core, (link, packed), (link_x, packed_x), work)


def first_tails_kernel(link, link_x, state_in, state, tails):
    _, core = place()
    ordered(True, core, link, link_x, lambda low, high: tails_of(low, high, state, tails))


def settle_gain(state, low, high, pair):
    high_gain = times_turned(state[GAIN_HIGH, pair], high[INVERSE, 2 * pair])
    low_gain = times_turned(state[GAIN_LOW, pair], low[INVERSE, 2 * pair])
    state[GAIN_HIGH, pair] = high_gain
    state[GAIN_LOW, pair] = low_gain - times_turned(high_gain, low[CHAIN, 2 * pair])


def even_gain_kernel(
    stage_of_turn, first, recv, link, link_x, forward, packed, packed_x, state_in, state
):
    stage, core = place()
    pairs = recv.shape[0]

    def work(low, high):
        if not first:
            for pair in range(pairs - 1):
                state[OUT_ODD_HIGH, pair] = state[REST_HIGH, pair] - times_turned(
                    recv[pair], high[0][CHAIN, 2 * pair + 1]
                )
        for layer, (blocks, links) in enumerate((low, high)):
            near, odd, gain = (
                (EVEN_LOW, OUT_ODD_LOW, GAIN_LOW),
                (EVEN_HIGH, OUT_ODD_HIGH, GAIN_HIGH),
            )[layer]
            for pair in range(pairs):
                fresh = forward[near, pair]
                if pair > 0:
                    fresh = fresh - link_of(links, 2 * pair - 1) * times_turned(
                        state[odd, pair - 1], blocks[SIDE, 2 * pair]
                    )
                fresh = fresh - link_of(links, 2 * pair) * times_turned(
                    state[odd, pair], blocks[SIDE, 2 * pair + 1]
                )
                state[gain, pair] = fresh
        for pair in range(1, pairs):
            settle_gain(state, low[0], high[0], pair)

    ordered(stage == stage_of_turn, core, (packed, link), (packed_x, link_x), work)


def even_first_kernel(stage_of_turn, tails, packed, packed_x, state_in, state):
    stage, core = place()

    def work(low, high):
        for layer, blocks in enumerate((low, high)):
            gain = (GAIN_LOW, GAIN_HIGH)[layer]
            state[gain, 0] = state[gain, 0] - times_turned(tails[layer], blocks[SIDE, 0])
        settle_gain(state, low, high, 0)

    ordered(stage == stage_of_turn, core, packed, packed_x, work)


def split_kernel(state, packed, packed_x, kept, sent):
    _, core = place()
    pairs = state.shape[1]

    def work(low, high):
        for pair in range(pairs):
            even_high = state[GAIN_HIGH, pair] - times_turned(
                state[EVEN_INFLOW, pair], high[CHAIN, 2 * pair]
            )
            if low is packed:
                kept[2 * pair] = state[OUT_EVEN_LOW, pair]
                kept[2 * pair + 1] = state[OUT_ODD_LOW, pair]
                sent[2 * pair] = even_high.astype(BF16)
                sent[2 * pair + 1] = state[OUT_ODD_HIGH, pair].astype(BF16)
            else:
                sent[2 * pair] = state[OUT_EVEN_LOW, pair].astype(BF16)
                sent[2 * pair + 1] = state[OUT_ODD_LOW, pair].astype(BF16)
                kept[2 * pair] = even_high
                kept[2 * pair + 1] = state[OUT_ODD_HIGH, pair]

    ordered(True, core, packed, packed_x, work)


def join_kernel(kept, arrived, result):
    _, core = place()
    cells, half = kept.shape[0], kept.shape[1]
    for cell in range(cells):
        result[cell, half_rows(core, half), :] = kept[cell]
        result[cell, half_rows(1 - core, half), :] = arrived[cell].astype(F32)


def shards(rhs, dinv, lower_up, lower_span, upper_down, upper_span, span_link):
    rhs, dinv, lower_up = rhs[0], dinv[0], lower_up[0]
    lower_span, upper_down, upper_span = lower_span[0], upper_down[0], upper_span[0]
    cells, vecs, width = rhs.shape
    pairs, half = cells // 2, vecs // 2
    streams, spans = lax.axis_size("stream"), lax.axis_size("span")
    last = streams // 2 - 1

    def swapped(value):
        return lax.ppermute(value, "stream", [(index, index ^ 1) for index in range(streams)])

    def hop(value, start, end):
        return lax.ppermute(
            value, "stream", [(2 * start + core, 2 * end + core) for core in (0, 1)]
        )

    def beside(value, stage, step):
        links = []
        for member in range(stage % SPAN_PERIOD, last + 1, SPAN_PERIOD):
            for core in (0, 1):
                for span in range(spans):
                    if 0 <= span + step < spans:
                        base = (2 * member + core) * spans + span
                        links.append((base, base + step))
        return lax.ppermute(value, ("stream", "span"), links)

    def in_hbm(value):
        return pltpu.with_memory_space_constraint(value, pltpu.HBM)

    def after(value, *others):
        return lax.optimization_barrier((value,) + others)[0]

    part = functools.partial
    vectors = ((pairs, half, width), BF16)
    edges = ((2, half, width), BF16)
    forward_shape = ((6, pairs, half, width), F32)
    backward_shape = ((8, pairs, half, width), F32)
    blocks = ((cells, width, width), BF16)
    packed_shape = ((cells, half, width), F32)
    lower_shape = ((pairs, width, width), BF16)

    source, packed, lower_even, lower_odd = run(
        load_kernel, [packed_shape, packed_shape, lower_shape, lower_shape],
        in_hbm(rhs), in_hbm(lower_up.reshape(pairs, 2, width, width)), hbm=(0, 1),
        scratch=[pltpu.SemaphoreType.DMA] * 4,
    )
    source_x = swapped(packed)
    lower_even_x = swapped(lower_even)
    lower_odd_x = swapped(after(lower_odd, source_x))
    side_x = swapped(after(lower_span, lower_even_x, source_x))
    link_x = swapped(after(span_link, lower_even_x))
    rows = (source, source_x)
    links = (span_link, link_x)
    evens = (lower_even, lower_even_x)
    odds = (lower_odd, lower_odd_x)
    sides = (lower_span, side_x)

    def even_turn(turn, recv, state):
        if turn == GATHER_TURN:
            state, out, packed = run(
                even_gather_kernel, [forward_shape, vectors, packed_shape], recv, both_even,
                *backs, state, early, alias={5: 0, 6: 2}, hbm=(2, 3, 4), **gathering,
            )
            packs.extend((packed, swapped(packed)))
        else:
            outs = [forward_shape, vectors][: 2 if turn < last else 1]
            state, *out = run(
                part(even_kernel, turn), outs, recv, both_even, state, alias={2: 0}
            )
            out = out[0] if turn < last else None
        sent = hop(out, turn, turn + 1) if turn < last else None
        state, heads = run(
            part(heads_kernel, turn), [forward_shape, edges], recv, *evens, state, alias={3: 0}
        )
        return state, sent, beside(heads, turn, -1)

    def odd_ready(turn, recv, heads, state):
        (state,) = run(
            part(odd_source_kernel, turn), [forward_shape], recv, *rows, *links, *evens, *odds,
            *sides, state, alias={11: 0},
        )
        (state,) = run(
            part(odd_last_kernel, turn), [forward_shape], heads, *links, *odds, *sides, state,
            alias={7: 0},
        )
        return state

    def odd_turn(turn, recv, state):
        outs = [forward_shape, vectors][: 2 if turn < last else 1]
        state, *out = run(part(odd_kernel, turn), outs, recv, both_odd, state, alias={2: 0})
        return state, hop(out[0], turn, turn + 1) if turn < last else None

    backs = (
        in_hbm(dinv), in_hbm(upper_down), in_hbm(upper_span.reshape(cells, width, width))
    )
    gathering = dict(
        scratch=[pltpu.VMEM((cells, width, width), BF16)] + [pltpu.SemaphoreType.DMA] * 3
    )
    packed_shape = ((3, cells, width, width), BF16)
    packs = []

    state, out = run(first_kernel, [forward_shape, vectors], *rows, *evens)
    even_recv = hop(out, 0, 1)
    state, heads = run(first_heads_kernel, [forward_shape, edges], state, alias={0: 0})
    heads = beside(heads, 0, -1)
    both_even, early = run(
        gather_early_kernel, [lower_shape, packed_shape], *evens, *backs, hbm=(2, 3, 4),
        **gathering,
    )
    here = even_recv
    state, even_recv, next_heads = even_turn(1, here, after(state, both_even))
    (state,) = run(
        part(odd_source_kernel, 0), [forward_shape], out, *rows, *links, *evens, *odds, *sides,
        state, alias={11: 0},
    )
    state, out = run(
        odd_finish_first_kernel, [forward_shape, vectors], heads, *links, *odds, *sides, state,
        alias={7: 0},
    )
    odd_recv = hop(out, 0, 1)
    state, both_odd = run(
        part(odd_source_ahead_kernel, 1), [forward_shape, lower_shape], here, *rows, *links,
        *evens, *odds, *sides, state, alias={11: 0},
    )
    state, out = run(
        part(odd_finish_kernel, 1), [forward_shape, vectors], next_heads, odd_recv, both_odd,
        *links, *odds, *sides, state, alias={9: 0},
    )
    odd_recv = hop(out, 1, 2)
    for turn in range(2, last):
        here = even_recv
        state, even_recv, heads = even_turn(turn, here, state)
        state = odd_ready(turn, here, heads, state)
        if turn == last - 1:
            here = even_recv
            state, _, heads = even_turn(last, here, state)
        state, odd_recv = odd_turn(turn, odd_recv, state)
    state = odd_ready(last, here, heads, state)
    forward, _ = odd_turn(last, odd_recv, state)

    def back_odd_turn(stage, recv, state):
        outs = [backward_shape, vectors][: 2 if stage > 0 else 1]
        state, *out = run(part(odd_low_kernel, stage), outs, recv, both_odd, state, alias={2: 0})
        sent = hop(out[0], stage, stage - 1) if stage > 0 else None
        state, tails = run(
            part(tails_kernel, stage), [backward_shape, edges], recv, *links, *packs, state,
            alias={5: 0},
        )
        return state, sent, beside(tails, stage, 1)

    def even_ready(stage, recv, tails, state):
        (state,) = run(
            part(even_gain_kernel, stage, stage == last), [backward_shape], recv, *links, forward,
            *packs, state, alias={6: 0},
        )
        (state,) = run(
            part(even_first_kernel, stage), [backward_shape], tails, *packs, state, alias={3: 0}
        )
        return state

    def back_even_turn(stage, recv, state):
        outs = [backward_shape, vectors][: 2 if stage > 0 else 1]
        state, *out = run(
            part(even_out_kernel, stage), outs, recv, both_even, state, alias={2: 0}
        )
        return state, hop(out[0], stage, stage - 1) if stage > 0 else None

    state, out = run(turn_back_kernel, [backward_shape, vectors], forward, *odds, *packs)
    odd_recv = hop(out, last, last - 1)
    state, tails = run(first_tails_kernel, [backward_shape, edges], *links, state, alias={2: 0})
    tails = beside(tails, last, 1)
    both_even, both_odd = run(part(back_product_kernel, last), [lower_shape] * 2, *packs)
    state = even_ready(last, out, tails, after(state, both_odd))
    state, out = run(first_even_out_kernel, [backward_shape, vectors], state, alias={0: 0})
    even_recv = hop(out, last, last - 1)
    for stage in range(last - 1, -1, -1):
        here = odd_recv
        state, odd_recv, tails = back_odd_turn(stage, here, state)
        state = even_ready(stage, here, tails, state)
        state, even_recv = back_even_turn(stage, even_recv, state)

    kept, sent = run(
        split_kernel, [((cells, half, width), F32), ((cells, half, width), BF16)], state, *packs
    )
    arrived = swapped(sent)
    in_vmem = pl.BlockSpec(memory_space=pltpu.VMEM)
    result = pl.pallas_call(
        join_kernel,
        out_shape=jax.ShapeDtypeStruct((cells, vecs, width), F32),
        in_specs=[in_vmem] * 2,
        out_specs=in_vmem,
        compiler_params=pltpu.CompilerParams(vmem_limit_bytes=LIMIT),
    )(kept, arrived)
    return result[None]


def solution(mesh):
    return jax.shard_map(
        shards,
        mesh=mesh,
        in_specs=(
            P("stream", "span", None, None),
            P("stream", "span", None, None),
            P("stream", "span", None, None),
            P("stream", "span", None, None, None),
            P("stream", "span", None, None),
            P("stream", "span", None, None, None),
            P("stream", "span"),
        ),
        out_specs=P("stream", "span", None, None),
        check_vma=False,
    )
```
